512 devices in a mesh: layer: 8 (over y, core), tile: 64 (over z, x).
Axes of the slice: x: 4, y: 4, z: 16, core: 2. Of those that a mesh axis runs over, the one named last changes fastest.
Arguments:
- cond_x: float32 [8, 256, 2048], P(None, 'tile', 'layer'), may hold values from 0.3 to 3
- cond_y: float32 [8, 256, 2048], P(None, 'tile', 'layer'), may hold values from 0.3 to 3
- via_cond: float32 [8, 256, 2048], P(None, 'tile', 'layer'), may hold values from 0.5 to 4
- capacity: float32 [8, 256, 2048], P(None, 'tile', 'layer'), may hold values from 0.002 to 0.02
- class_map: int32 [256, 2048], P('tile', 'layer'), may hold values from 0 to 7
- via_mask: int32 [8, 8], replicated, may hold values 0 or 1
- bank_map: int32 [8, 64, 128], P(None, 'tile', 'layer'), may hold values from 0 to 255
- source_late: float32 [8, 256, 2048], P(None, 'tile', 'layer'), may hold values from -6 to 6
- source_early: float32 [8, 256, 2048], P(None, 'tile', 'layer'), may hold values from -6 to 6
- rate_late: float32 [8, 256, 2048], P(None, 'tile', 'layer'), may hold values from -6 to 6
- rate_early: float32 [8, 256, 2048], P(None, 'tile', 'layer'), may hold values from -6 to 6
Outputs:
- adjoint_late: float32 [8, 256, 2048], P(None, 'tile', 'layer')
- adjoint_early: float32 [8, 256, 2048], P(None, 'tile', 'layer')
- bank_grad: float32 [256], replicated
The draws below stay inside these ranges and needn't reach their ends.
All inputs are finite; a program needn't handle non-finite values.
Results may differ from the reference program's by a relative error of at most 0.0003.
Values sent between devices are 32-bit elements; how exact they have to be, the bound alone decides.
A program may use at most 64 MiB of HBM per device.

```python
import math
import jax
import jax.numpy as jnp

COLS = 2048
LAYERS = 8
ITERS = 3
CHEB = 4
NCLASS = 8
DROWS = 4
DCOLS = 16
BANKS = 256
ROWS = 256


def touch_ends(values, stream_key, smallest, largest):
    shape = values.shape
    place = [jax.random.randint(jax.random.fold_in(stream_key, axis), (), 0, shape[axis]) for axis in range(len(shape))]
    values = values.at[tuple(place)].set(smallest)
    longest = shape.index(max(shape))
    place[longest] = (place[longest] + 1) % shape[longest]
    return values.at[tuple(place)].set(largest)


def steps_of(key, shape, pieces, least, high):
    factor_of = 1.0
    for position, shards_of in pieces:
        heights = jax.random.uniform(jax.random.fold_in(jax.random.fold_in(key, 6), position), (shards_of,), jnp.float32, least / len(pieces), high / len(pieces))
        factor_of = factor_of * jnp.repeat(jnp.exp(heights), shape[position] // shards_of).reshape((-1,) + (1,) * (len(shape) - 1 - position))
    return factor_of


def normal_values(stream_key, extent, deviation, most, split=(), held_as=jnp.bfloat16):
    values = jax.random.normal(stream_key, extent, jnp.float32) * deviation
    if len(split) > 0:
        values = steps_of(stream_key, extent, split, -0.22, 0.18) * values
    return jnp.clip(values, min=-most, max=most).astype(held_as)


def setup_inputs(seed: int = 0) -> dict:
    splits = jax.random.split(jax.random.key(seed), 12)
    cond_x = jnp.clip(jnp.exp(math.log(3.0) - 2.3025851 * jax.random.uniform(splits[0], (LAYERS, ROWS, COLS), jnp.float32) ** steps_of(splits[0], (LAYERS, ROWS, COLS), ((1, 64), (2, 8)), -0.2, 0.2)), 0.3, 3.0)
    cond_y = jnp.clip(jnp.exp(math.log(3.0) - 2.3025851 * jax.random.uniform(splits[1], (LAYERS, ROWS, COLS), jnp.float32) ** steps_of(splits[1], (LAYERS, ROWS, COLS), ((1, 64), (2, 8)), -0.2, 0.2)), 0.3, 3.0)
    via_cond = jnp.clip(jnp.exp(math.log(4.0) - 2.0794415 * jax.random.uniform(splits[2], (LAYERS, ROWS, COLS), jnp.float32) ** steps_of(splits[2], (LAYERS, ROWS, COLS), ((1, 64), (2, 8)), -0.2, 0.2)), 0.5, 4.0)
    capacity = jnp.clip(jnp.exp(math.log(0.02) - 2.30258502 * jax.random.uniform(splits[3], (LAYERS, ROWS, COLS), jnp.float32) ** steps_of(splits[3], (LAYERS, ROWS, COLS), ((1, 64), (2, 8)), -0.2, 0.2)), 0.002, 0.02)
    class_map = touch_ends(jax.random.randint(splits[4], (ROWS, COLS), 0, NCLASS), jax.random.fold_in(splits[4], 1), 0, NCLASS - 1).astype(jnp.int32)
    via_mask = touch_ends((jax.random.randint(splits[5], (LAYERS, NCLASS), 0, 2) < 1).astype(jnp.int32), jax.random.fold_in(splits[5], 1), 0, 1)
    bank_map = touch_ends(jax.random.randint(splits[6], (LAYERS, ROWS // DROWS, COLS // DCOLS), 0, BANKS), jax.random.fold_in(splits[6], 1), 0, BANKS - 1).astype(jnp.int32)
    source_late = normal_values(splits[7], (LAYERS, ROWS, COLS), 1.0, 6.0, ((1, 64), (2, 8)), jnp.float32)
    source_early = normal_values(splits[8], (LAYERS, ROWS, COLS), 1.0, 6.0, ((1, 64), (2, 8)), jnp.float32)
    rate_late = normal_values(splits[9], (LAYERS, ROWS, COLS), 1.0, 6.0, ((1, 64), (2, 8)), jnp.float32)
    rate_early = normal_values(splits[10], (LAYERS, ROWS, COLS), 1.0, 6.0, ((1, 64), (2, 8)), jnp.float32)
    return dict(cond_x=cond_x, cond_y=cond_y, via_cond=via_cond, capacity=capacity, class_map=class_map, via_mask=via_mask, bank_map=bank_map, source_late=source_late, source_early=source_early, rate_late=rate_late, rate_early=rate_early)


lower_edge = 0.05
upper_edge = 2.0
centre_value = (lower_edge + upper_edge) / 2.0
half_width = (upper_edge - lower_edge) / 2.0
sigma_value = centre_value / half_width


def couplings(cond_x, cond_y, via_cond, capacity, class_map, via_mask):
    east = cond_x.at[:, :, -1].set(0.0)
    west = jnp.pad(east[:, :, :-1], ((0, 0), (0, 0), (1, 0)))
    south = cond_y.at[:, -1, :].set(0.0)
    north = jnp.pad(south[:, :-1, :], ((0, 0), (1, 0), (0, 0)))
    opened = via_mask.astype(jnp.float32)[:, class_map]
    upward = (via_cond * opened).at[-1].set(0.0)
    downward = jnp.pad(upward[:-1], ((1, 0), (0, 0), (0, 0)))
    diagonal = capacity + east + west + south + north + upward + downward
    return east, west, south, north, upward, downward, diagonal


def operate(field, coefs):
    east, west, south, north, upward, downward, diagonal = coefs
    padded = jnp.pad(field, 1)
    result = diagonal * field - east * padded[1:-1, 1:-1, 2:] - west * padded[1:-1, 1:-1, :-2]
    result = result - south * padded[1:-1, 2:, 1:-1] - north * padded[1:-1, :-2, 1:-1]
    return result - upward * padded[2:, 1:-1, 1:-1] - downward * padded[:-2, 1:-1, 1:-1]


def precondition(residual, coefs):
    diagonal = coefs[6]
    smooth = residual / (centre_value * diagonal)
    step_dir = smooth
    rho_prev = 1.0 / sigma_value
    for sweep in range(CHEB - 1):
        rho_next = 1.0 / (2.0 * sigma_value - rho_prev)
        step_dir = rho_next * rho_prev * step_dir + (2.0 * rho_next / half_width) * (residual - operate(smooth, coefs)) / diagonal
        smooth = smooth + step_dir
        rho_prev = rho_next
    return smooth


def solve(rhs, coefs):
    solution = jnp.zeros_like(rhs)
    residual = rhs
    precond = precondition(residual, coefs)
    search = precond
    gamma = jnp.sum(residual * precond)
    for step in range(ITERS):
        image = operate(search, coefs)
        alpha = gamma / jnp.sum(search * image)
        solution = solution + alpha * search
        residual = residual - alpha * image
        if step + 1 < ITERS:
            precond = precondition(residual, coefs)
            gamma_next = jnp.sum(residual * precond)
            search = precond + (gamma_next / gamma) * search
            gamma = gamma_next
    return solution


def reference(cond_x, cond_y, via_cond, capacity, class_map, via_mask, bank_map, source_late, source_early, rate_late, rate_early):
    coefs = couplings(cond_x, cond_y, via_cond, capacity, class_map, via_mask)
    adjoint_late = solve(source_late, coefs)
    adjoint_early = solve(source_early + capacity * adjoint_late, coefs)
    product = adjoint_late * rate_late + adjoint_early * rate_early
    tiles = product.reshape(LAYERS, ROWS // DROWS, DROWS, COLS // DCOLS, DCOLS).sum(axis=(2, 4))
    bank_grad = jax.ops.segment_sum(tiles.reshape(-1), bank_map.reshape(-1), num_segments=BANKS)
    return adjoint_late, adjoint_early, bank_grad
```

```python
import functools

import jax
import jax.numpy as jnp
from jax import lax
from jax.experimental import pallas as pl
from jax.experimental.pallas import tpu as pltpu
from jax.sharding import PartitionSpec as P

MESH = pl.DeviceIdType.MESH
NCLASS = 8
DCOLS = 16
BANKS = 256
LAYERS = 8
ROWS = 4
COLS = 256
HALO = 4
SPAN = ROWS + 2 * HALO
WIDE = COLS + 128
FIELDS = 6
EAST, SOUTH, UP, CAP, LATE, EARLY = range(FIELDS)

lower_edge = 0.05
upper_edge = 2.0
centre = (lower_edge + upper_edge) / 2.0
half = (upper_edge - lower_edge) / 2.0
sigma = centre / half


def sweep_constants():
    out = []
    rho = 1.0 / sigma
    for _ in range(3):
        nxt = 1.0 / (2.0 * sigma - rho)
        out.append((nxt * rho, 2.0 * nxt / half))
        rho = nxt
    return out


def next_col(v):
    return pltpu.roll(v, WIDE - 1, 1)


def prev_col(v):
    return pltpu.roll(v, 1, 1)


def next_layer(v):
    return pltpu.roll(v, LAYERS - 1, 0)


def prev_layer(v):
    return pltpu.roll(v, 1, 0)


def neighbours(z, coef, r):
    v = z[r]
    acc = coef[0, r] * next_col(v) + coef[1, r] * prev_col(v)
    acc = acc + (coef[2, r] * z[r + 1] + coef[3, r] * z[r - 1])
    return acc + (coef[4, r] * next_layer(v) + coef[5, r] * prev_layer(v))


def krylov_coefficients(mu):
    zero = jnp.zeros_like(mu[0])
    one = zero + 1.0

    def form(c, base):
        total = None
        for s in range(2 * len(c) - 1):
            w = None
            for i in range(len(c)):
                j = s - i
                if 0 <= j < len(c):
                    w = c[i] * c[j] if w is None else w + c[i] * c[j]
            total = w * mu[base + s] if total is None else total + w * mu[base + s]
        return total

    res = [one]
    sea = [one]
    sol = [zero, zero, zero]
    gamma = mu[0]
    for step in range(3):
        alpha = gamma / form(sea, 1)
        sol = [s + alpha * sea[i] if i < len(sea) else s for i, s in enumerate(sol)]
        if step < 2:
            res = [
                (res[i] if i < len(res) else zero) - (alpha * sea[i - 1] if i > 0 else zero)
                for i in range(step + 2)
            ]
            new = form(res, 0)
            beta = new / gamma
            sea = [res[i] + (beta * sea[i] if i < len(sea) else zero) for i in range(step + 2)]
            gamma = new
    return sol


def kernel(
    cond_x, cond_y, via, cap, cls, mask, bank, late, early, rate_late, rate_early,
    out_late, out_early, out_bank,
    ext, col_r, col_l, sx, sx_r, sx_l, coef, diag, g, u, uh, z1, z2,
    a0, a1, a2, b0, b1, b2,
    halo_send, halo_recv, mid_send, mid_recv, ush_send, ush_recv, sum_send, sum_recv,
):
    lay = lax.axis_index("layer")
    til = lax.axis_index("tile")
    lays = lax.axis_size("layer")
    tils = lax.axis_size("tile")
    y, core = lay // 2, lay % 2
    z, x = til // 4, til % 4

    def at(dl, dt):
        return ((lay + dl + lays) % lays, (til + dt + tils) % tils)

    core_peer = [(lay + 1 - 2 * core, til)]
    plane_peers = [
        (((y + i // 4) % 4) * 2 + core, z * 4 + (x + i) % 4) for i in range(1, 16)
    ]
    z_peers = [(lay, ((z + i) % 16) * 4 + x) for i in range(1, 16)]

    barrier = pltpu.get_barrier_semaphore()
    greet = [at(dl, dt) for dt in (-2, -1, 0, 1, 2) for dl in (-1, 0, 1) if (dl, dt) != (0, 0)]
    greet += plane_peers + z_peers
    for d in greet:
        pl.semaphore_signal(barrier, inc=1, device_id=d, device_id_type=MESH)

    lane = lax.broadcasted_iota(jnp.int32, (LAYERS, COLS), 1)
    layer = lax.broadcasted_iota(jnp.int32, (LAYERS, COLS), 0)
    last_col = jnp.logical_and(lane == COLS - 1, lay == lays - 1)
    top = layer == LAYERS - 1
    masks = mask[...].astype(jnp.float32)
    for r in range(ROWS):
        e = HALO + r
        ext[EAST, e, :, :COLS] = jnp.where(last_col, 0.0, cond_x[:, r, :])
        south = cond_y[:, r, :]
        if r == ROWS - 1:
            south = jnp.where(til == tils - 1, 0.0, south)
        ext[SOUTH, e, :, :COLS] = south
        kind = jnp.broadcast_to(cls[r : r + 1, :], (LAYERS, COLS))
        opened = jnp.zeros((LAYERS, COLS), jnp.float32)
        for k in range(NCLASS):
            opened = jnp.where(kind == k, masks[:, k : k + 1], opened)
        ext[UP, e, :, :COLS] = jnp.where(top, 0.0, via[:, r, :] * opened)
        ext[CAP, e, :, :COLS] = cap[:, r, :]
        ext[LATE, e, :, :COLS] = late[:, r, :]
        ext[EARLY, e, :, :COLS] = early[:, r, :]

    pl.semaphore_wait(barrier, len(greet))

    own = pl.ds(HALO, ROWS)
    halo = []

    def send(src, dst, peer):
        n = len(halo)
        halo.append(
            pltpu.make_async_remote_copy(
                src_ref=src, dst_ref=dst, send_sem=halo_send.at[n], recv_sem=halo_recv.at[n],
                device_id=peer, device_id_type=MESH,
            )
        )
        halo[-1].start()

    for dt, row in ((1, 0), (-1, HALO + ROWS)):
        send(ext.at[:, own, :, pl.ds(0, COLS)], ext.at[:, pl.ds(row, HALO), :, pl.ds(0, COLS)], at(0, dt))
    for dt, row in ((1, 0), (-1, HALO + ROWS), (0, HALO)):
        send(ext.at[:, own, :, pl.ds(0, 128)], col_r.at[:, pl.ds(row, HALO)], at(-1, dt))
        send(ext.at[:, own, :, pl.ds(COLS - 128, 128)], col_l.at[:, pl.ds(row, HALO)], at(1, dt))
    far = ext.at[SOUTH, HALO + ROWS - 1]
    send(far.at[:, pl.ds(0, COLS)], sx.at[:, pl.ds(0, COLS)], at(0, 2))
    send(far.at[:, pl.ds(0, 128)], sx_r, at(-1, 2))
    send(far.at[:, pl.ds(COLS - 128, 128)], sx_l, at(1, 2))
    for c in halo:
        c.wait_recv()

    right = lax.broadcasted_iota(jnp.int32, (LAYERS, 128), 1) < 64
    for f in range(FIELDS):
        for r in range(SPAN):
            ext[f, r, :, COLS:] = jnp.where(right, col_r[f, r], col_l[f, r])
    north = jnp.concatenate([sx[...], jnp.where(right, sx_r[...], sx_l[...])], axis=1)
    for r in range(SPAN):
        east = ext[EAST, r]
        west = prev_col(east)
        south = ext[SOUTH, r]
        upward = ext[UP, r]
        downward = prev_layer(upward)
        d = ext[CAP, r] + east + west + south + north + upward + downward
        inv = 1.0 / d
        diag[0, r] = d
        diag[1, r] = inv
        g[0, r] = ext[LATE, r] * inv
        for i, c in enumerate((east, west, south, north, upward, downward)):
            coef[i, r] = c * inv
        north = south

    (q1, p1), (q2, p2), (q3, p3) = sweep_constants()

    def smooth(gi, ui):
        for r in range(1, SPAN - 1):
            z1[r] = ((1.0 + q1 - p1) / centre + p1) * gi[r] + (p1 / centre) * neighbours(gi, coef, r)
        for r in range(2, SPAN - 2):
            z2[r] = (1.0 + q2 - p2) * z1[r] + (p2 - q2 / centre) * gi[r] + p2 * neighbours(z1, coef, r)
        for r in range(3, SPAN - 3):
            ui[r] = (
                (1.0 + q3 - p3) * z2[r] - q3 * z1[r] + p3 * gi[r] + p3 * neighbours(z2, coef, r)
            )

    def rows_both_ways(ref, above, below, ssem, rsem):
        copies = []
        for n, (dt, dst) in enumerate(((1, above), (-1, below))):
            c = pltpu.make_async_remote_copy(
                src_ref=ref.at[own], dst_ref=dst,
                send_sem=ssem.at[n], recv_sem=rsem.at[n], device_id=at(0, dt), device_id_type=MESH,
            )
            c.start()
            copies.append(c)
        return copies

    pending = []

    def chain(base):
        parts = [None] * 6
        for i in range(3):
            gi, ui = g.at[base + i], u.at[base + i]
            smooth(gi, ui)
            gn = g.at[base + i + 1] if i < 2 else z1
            for r in range(HALO, HALO + ROWS):
                gn[r] = ui[r] - neighbours(ui, coef, r)
            if i < 2:
                k = base // 3 * 2 + i
                copies = rows_both_ways(
                    gn, gn.at[pl.ds(0, HALO)], gn.at[pl.ds(HALO + ROWS, HALO)],
                    mid_send.at[k], mid_recv.at[k],
                )
                pending.extend(copies)
            for r in range(HALO, HALO + ROWS):
                du = (diag[0, r] * ui[r])[:, :COLS]
                for k, ref in ((2 * i, gi), (2 * i + 1, gn)):
                    term = du * ref[r][:, :COLS]
                    parts[k] = term if parts[k] is None else parts[k] + term
            if i < 2:
                for c in copies:
                    c.wait_recv()
        lanes = lax.broadcasted_iota(jnp.int32, (1, 128), 1)
        row = jnp.zeros((1, 128), jnp.float32)
        for k, p in enumerate(parts):
            row = jnp.where(lanes == k, jnp.sum(p, axis=(0, 1), keepdims=True), row)
        return row

    def group_sum(buf, me, peers, n, ssem, rsem):
        for d in peers:
            pltpu.make_async_remote_copy(
                src_ref=buf.at[me], dst_ref=buf.at[me], send_sem=ssem, recv_sem=rsem,
                device_id=d, device_id_type=MESH,
            ).start()
        most = buf.at[pl.ds(0, n - 1)]
        whole = pltpu.make_async_remote_copy(
            src_ref=most, dst_ref=most, send_sem=ssem, recv_sem=rsem,
            device_id=peers[0], device_id_type=MESH,
        )
        whole.wait_recv()
        pending.append(whole)
        total = buf[0]
        for i in range(1, n):
            total = total + buf[i]
        return total

    def all_sum(bufs, base):
        c, p, w = bufs
        p[y * 4 + x] = group_sum(c, core, core_peer, 2, sum_send.at[base], sum_recv.at[base])
        w[z] = group_sum(p, y * 4 + x, plane_peers, 16, sum_send.at[base + 1], sum_recv.at[base + 1])
        return group_sum(w, z, z_peers, 16, sum_send.at[base + 2], sum_recv.at[base + 2])

    def coefficients(row):
        lanes = lax.broadcasted_iota(jnp.int32, (1, 128), 1)
        mu = [
            jnp.sum(jnp.where(lanes == k, row, 0.0), axis=(0, 1), keepdims=True) for k in range(6)
        ]
        return krylov_coefficients(mu)

    a0[core] = chain(0).reshape(1, 1, 128)
    for i in range(3):
        copies = rows_both_ways(
            u.at[i], uh.at[i, pl.ds(0, HALO)], uh.at[i, pl.ds(HALO, HALO)],
            ush_send.at[i], ush_recv.at[i],
        )
        pending.extend(copies)
    shadow = pending[-6:]
    c1 = coefficients(all_sum((a0, a1, a2), 0).reshape(1, 128))
    for c in shadow:
        c.wait_recv()
    held = jnp.zeros((LAYERS, COLS), jnp.float32)
    for r in range(SPAN):
        inside = HALO <= r < HALO + ROWS
        src, s = (u, r) if inside else (uh, r if r < HALO else r - ROWS)
        v = c1[0] * src[0, s] + c1[1] * src[1, s] + c1[2] * src[2, s]
        g[3, r] = (ext[EARLY, r] + ext[CAP, r] * v) * diag[1, r]
        if inside:
            out_late[:, r - HALO, :] = v[:, :COLS]
            held = held + v[:, :COLS] * rate_late[:, r - HALO, :]

    moments = chain(3)
    terms = [held]
    for i in range(3):
        t = None
        for r in range(ROWS):
            w = u[3 + i, HALO + r][:, :COLS] * rate_early[:, r, :]
            t = w if t is None else t + w
        terms.append(t)

    hi = lax.Precision.HIGHEST
    f32 = jnp.float32

    def iota(shape, dim):
        return lax.broadcasted_iota(jnp.int32, shape, dim)

    spread = (iota((16, 128), 0) == iota((16, 128), 1) % 16).astype(f32)
    bank_of = jnp.dot(bank[...].astype(f32), spread, precision=hi, preferred_element_type=f32)
    mine = iota((LAYERS, 128), 0) == iota((LAYERS, 128), 1) // 16
    bank_row = jnp.sum(jnp.where(mine, bank_of, 0.0), axis=0, keepdims=True)
    chosen = (iota((BANKS, 128), 0) == (bank_row + 0.5).astype(jnp.int32)).astype(f32)
    tile_of = (iota((COLS, 128), 0) // DCOLS == iota((COLS, 128), 1) % 16).astype(f32)
    tiles = jnp.dot(jnp.concatenate(terms, axis=0), tile_of, precision=hi, preferred_element_type=f32)
    tiles = jnp.where(iota((4 * LAYERS, 128), 0) % LAYERS == iota((4 * LAYERS, 128), 1) // 16, tiles, 0.0)
    sums = lax.dot_general(
        tiles, chosen, (((1,), (1,)), ((), ())), precision=hi, preferred_element_type=f32
    )
    for i in range(4):
        s = jnp.sum(sums[i * LAYERS : (i + 1) * LAYERS], axis=0, keepdims=True)
        b0[core, 2 * i] = s[:, :128]
        b0[core, 2 * i + 1] = s[:, 128:]
    b0[core, 8] = moments

    total = all_sum((b0, b1, b2), 3)
    c2 = coefficients(total[8])
    for h in range(2):
        out_bank[:, h * 128 : (h + 1) * 128] = (
            total[h] + c2[0] * total[2 + h] + c2[1] * total[4 + h] + c2[2] * total[6 + h]
        )
    for r in range(ROWS):
        e = HALO + r
        v = c2[0] * u[3, e] + c2[1] * u[4, e] + c2[2] * u[5, e]
        out_early[:, r, :] = v[:, :COLS]
    for c in halo:
        c.wait_send()
    for c in pending:
        c.wait_send()


def on_device(
    cond_x, cond_y, via_cond, capacity, class_map, via_mask, bank_map,
    source_late, source_early, rate_late, rate_early,
):
    f32 = jnp.float32
    vm = pl.BlockSpec(memory_space=pltpu.VMEM)
    dma = pltpu.SemaphoreType.DMA
    block = jax.ShapeDtypeStruct((LAYERS, ROWS, COLS), f32)
    wide = (SPAN, LAYERS, WIDE)
    late, early, bank = pl.pallas_call(
        kernel,
        out_shape=(block, block, jax.ShapeDtypeStruct((1, BANKS), f32)),
        in_specs=[vm] * 11,
        out_specs=(vm, vm, vm),
        scratch_shapes=[
            pltpu.VMEM((FIELDS,) + wide, f32),
            pltpu.VMEM((FIELDS, SPAN, LAYERS, 128), f32),
            pltpu.VMEM((FIELDS, SPAN, LAYERS, 128), f32),
            pltpu.VMEM((LAYERS, COLS), f32),
            pltpu.VMEM((LAYERS, 128), f32),
            pltpu.VMEM((LAYERS, 128), f32),
            pltpu.VMEM((6,) + wide, f32),
            pltpu.VMEM((2,) + wide, f32),
            pltpu.VMEM((6,) + wide, f32),
            pltpu.VMEM((6,) + wide, f32),
            pltpu.VMEM((3, 2 * HALO, LAYERS, WIDE), f32),
            pltpu.VMEM(wide, f32),
            pltpu.VMEM(wide, f32),
            pltpu.VMEM((2, 1, 1, 128), f32),
            pltpu.VMEM((16, 1, 1, 128), f32),
            pltpu.VMEM((16, 1, 1, 128), f32),
            pltpu.VMEM((2, 9, 1, 128), f32),
            pltpu.VMEM((16, 9, 1, 128), f32),
            pltpu.VMEM((16, 9, 1, 128), f32),
            dma((11,)),
            dma((11,)),
            dma((4, 2)),
            dma((4, 2)),
            dma((3, 2)),
            dma((3, 2)),
            dma((6,)),
            dma((6,)),
        ],
        compiler_params=pltpu.CompilerParams(
            collective_id=0, has_side_effects=True, vmem_limit_bytes=40 << 20
        ),
        name="adjoint_steps",
    )(
        cond_x, cond_y, via_cond, capacity, class_map, via_mask, bank_map.reshape(LAYERS, 16),
        source_late, source_early, rate_late, rate_early,
    )
    return late, early, bank.reshape(BANKS)


def solution(mesh):
    block = P(None, "tile", "layer")
    in_specs = (block,) * 4 + (P("tile", "layer"), P()) + (block,) * 5
    return jax.shard_map(
        on_device, mesh=mesh, in_specs=in_specs, out_specs=(block, block, P()), check_vma=False
    )
```

```python
import functools

import jax
import jax.numpy as jnp
from jax import lax
from jax.experimental import pallas as pl
from jax.experimental.pallas import tpu as pltpu
from jax.sharding import PartitionSpec as P

MESH = pl.DeviceIdType.MESH
NCLASS = 8
DCOLS = 16
BANKS = 256
LAYERS = 8
ROWS = 4
COLS = 256
HALO = 4
SPAN = ROWS + 2 * HALO
WIDE = COLS + 128
FIELDS = 6
EAST, SOUTH, UP, CAP, LATE, EARLY = range(FIELDS)

lower_edge = 0.05
upper_edge = 2.0
centre = (lower_edge + upper_edge) / 2.0
half = (upper_edge - lower_edge) / 2.0
sigma = centre / half


def sweep_constants():
    out = []
    rho = 1.0 / sigma
    for _ in range(3):
        nxt = 1.0 / (2.0 * sigma - rho)
        out.append((nxt * rho, 2.0 * nxt / half))
        rho = nxt
    return out


def next_col(v):
    return pltpu.roll(v, WIDE - 1, 1)


def prev_col(v):
    return pltpu.roll(v, 1, 1)


def next_layer(v):
    return pltpu.roll(v, LAYERS - 1, 0)


def prev_layer(v):
    return pltpu.roll(v, 1, 0)


def neighbours(z, coef, r):
    v = z[r]
    acc = coef[0, r] * next_col(v) + coef[1, r] * prev_col(v)
    acc = acc + (coef[2, r] * z[r + 1] + coef[3, r] * z[r - 1])
    return acc + (coef[4, r] * next_layer(v) + coef[5, r] * prev_layer(v))


def krylov_coefficients(mu):
    zero = jnp.zeros_like(mu[0])
    one = zero + 1.0
    nu = [mu[s] - mu[s + 1] for s in range(5)]

    def form(c, moments):
        total = None
        for s in range(2 * len(c) - 1):
            w = None
            for i in range(len(c)):
                j = s - i
                if 0 <= j < len(c):
                    w = c[i] * c[j] if w is None else w + c[i] * c[j]
            total = w * moments[s] if total is None else total + w * moments[s]
        return total

    def plus(a, b, scale):
        n = max(len(a), len(b))
        a, b = a + [zero] * (n - len(a)), b + [zero] * (n - len(b))
        return [p + scale * q for p, q in zip(a, b)]

    res, sea, sol = [one], [one], []
    gamma = mu[0]
    for step in range(3):
        alpha = gamma / form(sea, nu)
        sol = plus(sol, sea, alpha)
        if step < 2:
            res = plus(plus(res, sea, -alpha), [zero] + sea, alpha)
            new = form(res, mu)
            sea = plus(res, sea, new / gamma)
            gamma = new
    return sol


def kernel(
    cond_x_in, cond_y_in, via_in, cap_in, cls_in, mask_in, bank_in, late_in, early_in, rate_late_in, rate_early_in,
    late_out, early_out, bank_out,
    out_late, out_early, out_bank, cond_x, cond_y, via, cap, cls, mask, bank, late, early, rate_late, rate_early,
    ext, col_r, col_l, sx, sx_r, sx_l, coef, diag, g, u, uh, z1, z2,
    a0, a1, a2, b0, b1, b2,
    load_sem, store_sem, halo_send, halo_recv, mid_send, mid_recv, ush_send, ush_recv, sum_send, sum_recv, reach,
):
    loads = [
        pltpu.make_async_copy(src, dst, load_sem.at[n])
        for n, (src, dst) in enumerate((
            (cond_x_in, cond_x), (cond_y_in, cond_y), (via_in, via), (cap_in, cap), (cls_in, cls),
            (mask_in, mask), (late_in, late), (early_in, early), (bank_in, bank),
            (rate_late_in, rate_late), (rate_early_in, rate_early),
        ))
    ]
    for c in loads:
        c.start()

    lay = lax.axis_index("layer")
    til = lax.axis_index("tile")
    lays = lax.axis_size("layer")
    tils = lax.axis_size("tile")
    y, core = lay // 2, lay % 2
    z, x = til // 4, til % 4

    def at(dl, dt):
        return ((lay + dl + lays) % lays, (til + dt + tils) % tils)

    core_peer = [(lay + 1 - 2 * core, til)]
    plane_peers = [
        (((y + i // 4) % 4) * 2 + core, z * 4 + (x + i) % 4) for i in range(1, 16)
    ]
    z_peers = [(lay, ((z + i) % 16) * 4 + x) for i in range(1, 16)]

    barrier = pltpu.get_barrier_semaphore()
    greet = [at(dl, dt) for dt in (-2, -1, 0, 1, 2) for dl in (-1, 0, 1) if (dl, dt) != (0, 0)]
    greet += plane_peers + [at(0, 4 * dz) for dz in (-2, -1, 1, 2)]
    for d in greet:
        pl.semaphore_signal(barrier, inc=1, device_id=d, device_id_type=MESH)

    lane = lax.broadcasted_iota(jnp.int32, (LAYERS, COLS), 1)
    layer = lax.broadcasted_iota(jnp.int32, (LAYERS, COLS), 0)
    last_col = jnp.logical_and(lane == COLS - 1, lay == lays - 1)
    top = layer == LAYERS - 1
    for c in loads[:8]:
        c.wait()
    masks = mask[...].astype(jnp.float32)
    for r in range(ROWS):
        e = HALO + r
        ext[EAST, e, :, :COLS] = jnp.where(last_col, 0.0, cond_x[:, r, :])
        south = cond_y[:, r, :]
        if r == ROWS - 1:
            south = jnp.where(til == tils - 1, 0.0, south)
        ext[SOUTH, e, :, :COLS] = south
        kind = jnp.broadcast_to(cls[r : r + 1, :], (LAYERS, COLS))
        opened = jnp.zeros((LAYERS, COLS), jnp.float32)
        for k in range(NCLASS):
            opened = jnp.where(kind == k, masks[:, k : k + 1], opened)
        ext[UP, e, :, :COLS] = jnp.where(top, 0.0, via[:, r, :] * opened)
        ext[CAP, e, :, :COLS] = cap[:, r, :]
        ext[LATE, e, :, :COLS] = late[:, r, :]
        ext[EARLY, e, :, :COLS] = early[:, r, :]

    pl.semaphore_wait(barrier, len(greet))
    for dz in (-2, 2):
        pl.semaphore_signal(reach.at[0], inc=1, device_id=at(0, 4 * dz), device_id_type=MESH)

    own = pl.ds(HALO, ROWS)
    halo = []

    def send(src, dst, peer):
        n = len(halo)
        halo.append(
            pltpu.make_async_remote_copy(
                src_ref=src, dst_ref=dst, send_sem=halo_send.at[n], recv_sem=halo_recv.at[n],
                device_id=peer, device_id_type=MESH,
            )
        )
        halo[-1].start()

    def send_fields(first, count):
        fields = pl.ds(first, count)
        for dt, row in ((1, 0), (-1, HALO + ROWS)):
            send(
                ext.at[fields, own, :, pl.ds(0, COLS)],
                ext.at[fields, pl.ds(row, HALO), :, pl.ds(0, COLS)],
                at(0, dt),
            )
        for dt, row in ((1, 0), (-1, HALO + ROWS), (0, HALO)):
            send(ext.at[fields, own, :, pl.ds(0, 128)], col_r.at[fields, pl.ds(row, HALO)], at(-1, dt))
            send(
                ext.at[fields, own, :, pl.ds(COLS - 128, 128)],
                col_l.at[fields, pl.ds(row, HALO)],
                at(1, dt),
            )

    send_fields(0, EARLY)
    far = ext.at[SOUTH, HALO + ROWS - 1]
    send(far.at[:, pl.ds(0, COLS)], sx.at[:, pl.ds(0, COLS)], at(0, 2))
    send(far.at[:, pl.ds(0, 128)], sx_r, at(-1, 2))
    send(far.at[:, pl.ds(COLS - 128, 128)], sx_l, at(1, 2))
    first = len(halo)
    send_fields(EARLY, 1)
    for c in halo[:first]:
        c.wait_recv()
    pl.semaphore_wait(reach.at[0], 2)
    for dz in (-4, 4):
        pl.semaphore_signal(reach.at[1], inc=1, device_id=at(0, 4 * dz), device_id_type=MESH)

    right = lax.broadcasted_iota(jnp.int32, (LAYERS, 128), 1) < 64
    def merge_columns(f):
        for r in range(SPAN):
            ext[f, r, :, COLS:] = jnp.where(right, col_r[f, r], col_l[f, r])

    for f in range(EARLY):
        merge_columns(f)
    north = jnp.concatenate([sx[...], jnp.where(right, sx_r[...], sx_l[...])], axis=1)
    for r in range(SPAN):
        east = ext[EAST, r]
        west = prev_col(east)
        south = ext[SOUTH, r]
        upward = ext[UP, r]
        downward = prev_layer(upward)
        d = ext[CAP, r] + east + west + south + north + upward + downward
        inv = 1.0 / d
        diag[0, r] = d
        diag[1, r] = inv
        g[0, r] = ext[LATE, r] * inv
        for i, c in enumerate((east, west, south, north, upward, downward)):
            coef[i, r] = c * inv
        north = south

    (q1, p1), (q2, p2), (q3, p3) = sweep_constants()

    def smooth(gi, ui):
        for r in range(1, SPAN - 1):
            z1[r] = ((1.0 + q1 - p1) / centre + p1) * gi[r] + (p1 / centre) * neighbours(gi, coef, r)
        for r in range(2, SPAN - 2):
            z2[r] = (1.0 + q2 - p2) * z1[r] + (p2 - q2 / centre) * gi[r] + p2 * neighbours(z1, coef, r)
        for r in range(3, SPAN - 3):
            ui[r] = (
                (1.0 + q3 - p3) * z2[r] - q3 * z1[r] + p3 * gi[r] + p3 * neighbours(z2, coef, r)
            )

    def rows_both_ways(ref, above, below, ssem, rsem):
        copies = []
        for n, (dt, dst) in enumerate(((1, above), (-1, below))):
            c = pltpu.make_async_remote_copy(
                src_ref=ref.at[own], dst_ref=dst,
                send_sem=ssem.at[n], recv_sem=rsem.at[n], device_id=at(0, dt), device_id_type=MESH,
            )
            c.start()
            copies.append(c)
        return copies

    pending = []

    def chain(base):
        parts = [None] * 6
        for i in range(3):
            gi, ui = g.at[base + i], u.at[base + i]
            smooth(gi, ui)
            gn = g.at[base + i + 1] if i < 2 else z1
            for r in range(HALO, HALO + ROWS):
                gn[r] = gi[r] - ui[r] + neighbours(ui, coef, r)
            if i < 2:
                k = base // 3 * 2 + i
                copies = rows_both_ways(
                    gn, gn.at[pl.ds(0, HALO)], gn.at[pl.ds(HALO + ROWS, HALO)],
                    mid_send.at[k], mid_recv.at[k],
                )
                pending.extend(copies)
            for r in range(HALO, HALO + ROWS):
                du = (diag[0, r] * ui[r])[:, :COLS]
                for k, ref in ((2 * i, gi), (2 * i + 1, gn)):
                    term = du * ref[r][:, :COLS]
                    parts[k] = term if parts[k] is None else parts[k] + term
            if i < 2:
                for c in copies:
                    c.wait_recv()
        lanes = lax.broadcasted_iota(jnp.int32, (1, 128), 1)
        row = jnp.zeros((1, 128), jnp.float32)
        for k, p in enumerate(parts):
            row = jnp.where(lanes == k, jnp.sum(p, axis=(0, 1), keepdims=True), row)
        return row

    def group_sum(buf, me, peers, n, ssem, rsem):
        for d in peers:
            pltpu.make_async_remote_copy(
                src_ref=buf.at[me], dst_ref=buf.at[me], send_sem=ssem, recv_sem=rsem,
                device_id=d, device_id_type=MESH,
            ).start()
        most = buf.at[pl.ds(0, n - 1)]
        whole = pltpu.make_async_remote_copy(
            src_ref=most, dst_ref=most, send_sem=ssem, recv_sem=rsem,
            device_id=peers[0], device_id_type=MESH,
        )
        whole.wait_recv()
        pending.append(whole)
        total = buf[0]
        for i in range(1, n):
            total = total + buf[i]
        return total

    def all_sum(bufs, base):
        c, p, w = bufs
        p[y * 4 + x] = group_sum(c, core, core_peer, 2, sum_send.at[base], sum_recv.at[base])
        w[z] = group_sum(p, y * 4 + x, plane_peers, 16, sum_send.at[base + 1], sum_recv.at[base + 1])
        return group_sum(w, z, z_peers, 16, sum_send.at[base + 2], sum_recv.at[base + 2])

    def coefficients(row):
        lanes = lax.broadcasted_iota(jnp.int32, (1, 128), 1)
        mu = [
            jnp.sum(jnp.where(lanes == k, row, 0.0), axis=(0, 1), keepdims=True) for k in range(6)
        ]
        return krylov_coefficients(mu)

    a0[core] = chain(0).reshape(1, 1, 128)
    for i in range(3):
        copies = rows_both_ways(
            u.at[i], uh.at[i, pl.ds(0, HALO)], uh.at[i, pl.ds(HALO, HALO)],
            ush_send.at[i], ush_recv.at[i],
        )
        pending.extend(copies)
    shadow = pending[-6:]
    for c in halo[first:]:
        c.wait_recv()
    merge_columns(EARLY)
    pl.semaphore_wait(reach.at[1], 2)
    for c in loads[8:10]:
        c.wait()
    c1 = coefficients(all_sum((a0, a1, a2), 0).reshape(1, 128))
    for c in shadow:
        c.wait_recv()
    held = jnp.zeros((LAYERS, COLS), jnp.float32)
    for r in range(SPAN):
        inside = HALO <= r < HALO + ROWS
        src, s = (u, r) if inside else (uh, r if r < HALO else r - ROWS)
        v = c1[0] * src[0, s] + c1[1] * src[1, s] + c1[2] * src[2, s]
        g[3, r] = (ext[EARLY, r] + ext[CAP, r] * v) * diag[1, r]
        if inside:
            out_late[:, r - HALO, :] = v[:, :COLS]
            held = held + v[:, :COLS] * rate_late[:, r - HALO, :]

    stores = [
        pltpu.make_async_copy(src, dst, store_sem.at[n])
        for n, (src, dst) in enumerate(
            ((out_late, late_out), (out_early, early_out), (out_bank, bank_out))
        )
    ]
    stores[0].start()

    for c in loads[10:]:
        c.wait()
    moments = chain(3)
    terms = [held]
    for i in range(3):
        t = None
        for r in range(ROWS):
            w = u[3 + i, HALO + r][:, :COLS] * rate_early[:, r, :]
            t = w if t is None else t + w
        terms.append(t)

    hi = lax.Precision.HIGHEST
    f32 = jnp.float32

    def iota(shape, dim):
        return lax.broadcasted_iota(jnp.int32, shape, dim)

    spread = (iota((16, 128), 0) == iota((16, 128), 1) % 16).astype(f32)
    bank_of = jnp.dot(bank[...].astype(f32), spread, precision=hi, preferred_element_type=f32)
    mine = iota((LAYERS, 128), 0) == iota((LAYERS, 128), 1) // 16
    bank_row = jnp.sum(jnp.where(mine, bank_of, 0.0), axis=0, keepdims=True)
    chosen = (iota((BANKS, 128), 0) == (bank_row + 0.5).astype(jnp.int32)).astype(f32)
    tile_of = (iota((COLS, 128), 0) // DCOLS == iota((COLS, 128), 1) % 16).astype(f32)
    tiles = jnp.dot(jnp.concatenate(terms, axis=0), tile_of, precision=hi, preferred_element_type=f32)
    tiles = jnp.where(iota((4 * LAYERS, 128), 0) % LAYERS == iota((4 * LAYERS, 128), 1) // 16, tiles, 0.0)
    sums = lax.dot_general(
        tiles, chosen, (((1,), (1,)), ((), ())), precision=hi, preferred_element_type=f32
    )
    for i in range(4):
        s = jnp.sum(sums[i * LAYERS : (i + 1) * LAYERS], axis=0, keepdims=True)
        b0[core, 2 * i] = s[:, :128]
        b0[core, 2 * i + 1] = s[:, 128:]
    b0[core, 8] = moments

    total = all_sum((b0, b1, b2), 3)
    c2 = coefficients(total[8])
    for h in range(2):
        out_bank[:, h * 128 : (h + 1) * 128] = (
            total[h] + c2[0] * total[2 + h] + c2[1] * total[4 + h] + c2[2] * total[6 + h]
        )
    for r in range(ROWS):
        e = HALO + r
        v = c2[0] * u[3, e] + c2[1] * u[4, e] + c2[2] * u[5, e]
        out_early[:, r, :] = v[:, :COLS]
    stores[1].start()
    stores[2].start()
    for c in halo:
        c.wait_send()
    for c in pending:
        c.wait_send()
    for c in stores:
        c.wait()


def finish(late, early, bank, out_late, out_early, out_bank, sem):
    copies = [
        pltpu.make_async_copy(src, dst, sem.at[n])
        for n, (src, dst) in enumerate(((late, out_late), (early, out_early), (bank, out_bank)))
    ]
    for c in copies:
        c.start()
    for c in copies:
        c.wait()


def on_device(
    cond_x, cond_y, via_cond, capacity, class_map, via_mask, bank_map,
    source_late, source_early, rate_late, rate_early,
):
    f32, i32 = jnp.float32, jnp.int32
    hbm = pl.BlockSpec(memory_space=pltpu.HBM)
    dma = pltpu.SemaphoreType.DMA
    block = jax.ShapeDtypeStruct((LAYERS, ROWS, COLS), f32)
    shapes = (block, block, jax.ShapeDtypeStruct((1, BANKS), f32))
    wide = (SPAN, LAYERS, WIDE)
    field = pltpu.VMEM((LAYERS, ROWS, COLS), f32)
    results = pl.pallas_call(
        kernel,
        out_shape=shapes,
        in_specs=[hbm] * 11,
        out_specs=(hbm,) * 3,
        scratch_shapes=[
            field, field, pltpu.VMEM((1, BANKS), f32),
            field, field, field, field,
            pltpu.VMEM((ROWS, COLS), i32),
            pltpu.VMEM((LAYERS, NCLASS), i32),
            pltpu.VMEM((LAYERS, 16), i32),
            field, field, field, field,
            pltpu.VMEM((FIELDS,) + wide, f32),
            pltpu.VMEM((FIELDS, SPAN, LAYERS, 128), f32),
            pltpu.VMEM((FIELDS, SPAN, LAYERS, 128), f32),
            pltpu.VMEM((LAYERS, COLS), f32),
            pltpu.VMEM((LAYERS, 128), f32),
            pltpu.VMEM((LAYERS, 128), f32),
            pltpu.VMEM((6,) + wide, f32),
            pltpu.VMEM((2,) + wide, f32),
            pltpu.VMEM((6,) + wide, f32),
            pltpu.VMEM((6,) + wide, f32),
            pltpu.VMEM((3, 2 * HALO, LAYERS, WIDE), f32),
            pltpu.VMEM(wide, f32),
            pltpu.VMEM(wide, f32),
            pltpu.VMEM((2, 1, 1, 128), f32),
            pltpu.VMEM((16, 1, 1, 128), f32),
            pltpu.VMEM((16, 1, 1, 128), f32),
            pltpu.VMEM((2, 9, 1, 128), f32),
            pltpu.VMEM((16, 9, 1, 128), f32),
            pltpu.VMEM((16, 9, 1, 128), f32),
            dma((11,)),
            dma((3,)),
            dma((19,)),
            dma((19,)),
            dma((4, 2)),
            dma((4, 2)),
            dma((3, 2)),
            dma((3, 2)),
            dma((6,)),
            dma((6,)),
            pltpu.SemaphoreType.REGULAR((2,)),
        ],
        compiler_params=pltpu.CompilerParams(
            collective_id=0, has_side_effects=True, vmem_limit_bytes=60 << 20
        ),
        name="adjoint_steps",
    )(
        cond_x, cond_y, via_cond, capacity, class_map, via_mask, bank_map.reshape(LAYERS, 16),
        source_late, source_early, rate_late, rate_early,
    )
    late, early, bank = pl.pallas_call(
        finish,
        out_shape=shapes,
        in_specs=[hbm] * 3,
        out_specs=(hbm,) * 3,
        scratch_shapes=[dma((3,))],
        compiler_params=pltpu.CompilerParams(vmem_limit_bytes=60 << 20),
        name="write_results",
    )(*results)
    return late, early, bank.reshape(BANKS)


def solution(mesh):
    block = P(None, "tile", "layer")
    in_specs = (block,) * 4 + (P("tile", "layer"), P()) + (block,) * 5
    return jax.shard_map(
        on_device, mesh=mesh, in_specs=in_specs, out_specs=(block, block, P()), check_vma=False
    )
```

```python
import functools

import jax
import jax.numpy as jnp
from jax import lax
from jax.experimental import pallas as pl
from jax.experimental.pallas import tpu as pltpu
from jax.sharding import PartitionSpec as P

MESH = pl.DeviceIdType.MESH
NCLASS = 8
DCOLS = 16
BANKS = 256
LAYERS = 8
ROWS = 4
COLS = 256
HALO = 8
NEAR = 4
SPAN = ROWS + 2 * HALO
WIDE = COLS + 128
EDGE = 24
FIELDS = 6
EAST, SOUTH, UP, CAP, LATE, EARLY = range(FIELDS)

lower_edge = 0.05
upper_edge = 2.0
centre = (lower_edge + upper_edge) / 2.0
half = (upper_edge - lower_edge) / 2.0
sigma = centre / half


def sweep_constants():
    out = []
    rho = 1.0 / sigma
    for _ in range(3):
        nxt = 1.0 / (2.0 * sigma - rho)
        out.append((nxt * rho, 2.0 * nxt / half))
        rho = nxt
    return out


def next_col(v):
    return pltpu.roll(v, WIDE - 1, 1)


def prev_col(v):
    return pltpu.roll(v, 1, 1)


def next_layer(v):
    return pltpu.roll(v, LAYERS - 1, 0)


def prev_layer(v):
    return pltpu.roll(v, 1, 0)


def neighbours(z, coef, r):
    v = z[r]
    acc = coef[0, r] * next_col(v) + coef[1, r] * prev_col(v)
    acc = acc + (coef[2, r] * z[r + 1] + coef[3, r] * z[r - 1])
    return acc + (coef[4, r] * next_layer(v) + coef[5, r] * prev_layer(v))


def krylov_coefficients(mu):
    zero = jnp.zeros_like(mu[0])
    one = zero + 1.0
    nu = [mu[s] - mu[s + 1] for s in range(5)]

    def form(c, moments):
        total = None
        for s in range(2 * len(c) - 1):
            w = None
            for i in range(len(c)):
                j = s - i
                if 0 <= j < len(c):
                    w = c[i] * c[j] if w is None else w + c[i] * c[j]
            total = w * moments[s] if total is None else total + w * moments[s]
        return total

    def plus(a, b, scale):
        n = max(len(a), len(b))
        a, b = a + [zero] * (n - len(a)), b + [zero] * (n - len(b))
        return [p + scale * q for p, q in zip(a, b)]

    res, sea, sol = [one], [one], []
    gamma = mu[0]
    for step in range(3):
        alpha = gamma / form(sea, nu)
        sol = plus(sol, sea, alpha)
        if step < 2:
            res = plus(plus(res, sea, -alpha), [zero] + sea, alpha)
            new = form(res, mu)
            sea = plus(res, sea, new / gamma)
            gamma = new
    return sol


def kernel(
    cond_x_in, cond_y_in, via_in, cap_in, cls_in, mask_in, bank_in, late_in, early_in, rate_late_in, rate_early_in,
    late_out, early_out, bank_out,
    out_late, out_early, out_bank, cond_x, cond_y, via, cap, cls, mask, bank, late, early, rate_late, rate_early,
    ext, pack_r, pack_l, col_r, col_l, early_r, early_l, sx, sx_r, sx_l, coef, diag, g, u, uh, z1, z2,
    a0, a1, a2, b0, b1, b2,
    load_sem, store_sem, halo_send, halo_recv, mid_send, mid_recv, ush_send, ush_recv, sum_send, sum_recv, reach,
):
    loads = [
        pltpu.make_async_copy(src, dst, load_sem.at[n])
        for n, (src, dst) in enumerate((
            (cond_x_in, cond_x), (cond_y_in, cond_y), (via_in, via), (cap_in, cap), (cls_in, cls),
            (mask_in, mask), (late_in, late), (early_in, early), (bank_in, bank),
            (rate_late_in, rate_late), (rate_early_in, rate_early),
        ))
    ]
    for c in loads:
        c.start()

    lay = lax.axis_index("layer")
    til = lax.axis_index("tile")
    lays = lax.axis_size("layer")
    tils = lax.axis_size("tile")
    y, core = lay // 2, lay % 2
    z, x = til // 4, til % 4

    def at(dl, dt):
        return ((lay + dl + lays) % lays, (til + dt + tils) % tils)

    core_peer = [(lay + 1 - 2 * core, til)]
    plane_peers = [
        (((y + dy) % 4) * 2 + core, z * 4 + (x + dx) % 4)
        for dy in (2, 1, 3, 0) for dx in (2, 1, 3, 0) if (dy, dx) != (0, 0)
    ]
    z_peers = [
        (lay, ((z + i) % 16) * 4 + x) for i in sorted(range(1, 16), key=lambda i: -min(i, 16 - i))
    ]

    barrier = pltpu.get_barrier_semaphore()
    greet = [at(dl, dt) for dt in (-2, -1, 0, 1, 2) for dl in (-1, 0, 1) if (dl, dt) != (0, 0)]
    greet += plane_peers + [at(0, 4 * dz) for dz in (-2, 2, -1, 1)]
    for d in greet:
        pl.semaphore_signal(barrier, inc=1, device_id=d, device_id_type=MESH)

    lane = lax.broadcasted_iota(jnp.int32, (LAYERS, COLS), 1)
    layer = lax.broadcasted_iota(jnp.int32, (LAYERS, COLS), 0)
    last_col = jnp.logical_and(lane == COLS - 1, lay == lays - 1)
    top = layer == LAYERS - 1
    for c in loads[:8]:
        c.wait()
    masks = mask[...].astype(jnp.float32)
    for r in range(ROWS):
        e = HALO + r
        ext[EAST, e, :, :COLS] = jnp.where(last_col, 0.0, cond_x[:, r, :])
        south = cond_y[:, r, :]
        if r == ROWS - 1:
            south = jnp.where(til == tils - 1, 0.0, south)
        ext[SOUTH, e, :, :COLS] = south
        kind = jnp.broadcast_to(cls[r : r + 1, :], (LAYERS, COLS))
        opened = jnp.zeros((LAYERS, COLS), jnp.float32)
        for k in range(NCLASS):
            opened = jnp.where(kind == k, masks[:, k : k + 1], opened)
        ext[UP, e, :, :COLS] = jnp.where(top, 0.0, via[:, r, :] * opened)
        ext[CAP, e, :, :COLS] = cap[:, r, :]
        ext[LATE, e, :, :COLS] = late[:, r, :]
        ext[EARLY, e, :, :COLS] = early[:, r, :]
        lane128 = lax.broadcasted_iota(jnp.int32, (LAYERS, 128), 1)
        right = jnp.zeros((LAYERS, 128), jnp.float32)
        left = right
        for f in range(EARLY):
            here = jnp.logical_and(lane128 >= EDGE * f, lane128 < EDGE * (f + 1))
            v = ext[f, e, :, :128]
            right = jnp.where(here, pltpu.roll(v, EDGE * f, 1) if f else v, right)
            v = ext[f, e, :, COLS - 128 : COLS]
            left = jnp.where(here, pltpu.roll(v, (EDGE * (f + 1)) % 128, 1), left)
        pack_r[r] = right
        pack_l[r] = left

    pl.semaphore_wait(barrier, len(greet))
    for dz in (-2, 2):
        pl.semaphore_signal(reach.at[0], inc=1, device_id=at(0, 4 * dz), device_id_type=MESH)

    own = pl.ds(HALO, ROWS)
    halo = []

    def send(src, dst, peer):
        n = len(halo)
        halo.append(
            pltpu.make_async_remote_copy(
                src_ref=src, dst_ref=dst, send_sem=halo_send.at[n], recv_sem=halo_recv.at[n],
                device_id=peer, device_id_type=MESH,
            )
        )
        halo[-1].start()

    def send_rows(first, count, dt, row):
        fields = pl.ds(first, count)
        send(
            ext.at[fields, own, :, pl.ds(0, COLS)],
            ext.at[fields, pl.ds(row, ROWS), :, pl.ds(0, COLS)],
            at(0, dt),
        )

    def send_columns(dt, row):
        send(pack_r, col_r.at[pl.ds(row, ROWS)], at(-1, dt))
        send(pack_l, col_l.at[pl.ds(row, ROWS)], at(1, dt))

    near = ((1, HALO - NEAR), (-1, HALO + ROWS))
    far = ((2, 0), (-2, HALO + ROWS + NEAR))
    last = ext.at[SOUTH, HALO + ROWS - 1]
    send(last.at[:, pl.ds(0, 128)], sx_r, at(-1, 2))
    send(last.at[:, pl.ds(COLS - 128, 128)], sx_l, at(1, 2))
    send(last.at[:, pl.ds(0, COLS)], sx, at(0, 2))
    for dt, row in near:
        send_columns(dt, row)
    for dt, row in near:
        send_rows(0, EARLY, dt, row)
    send_columns(0, HALO)
    first = len(halo)
    for c in halo:
        c.wait_recv()
    for dt, row in far:
        send_rows(0, LATE, dt, row)
        send_columns(dt, row)
    second = len(halo)
    for dt, row in near + ((0, HALO),):
        if dt:
            send_rows(EARLY, 1, dt, row)
        send(ext.at[EARLY, own, :, pl.ds(0, 128)], early_r.at[pl.ds(row, ROWS)], at(-1, dt))
        send(
            ext.at[EARLY, own, :, pl.ds(COLS - 128, 128)], early_l.at[pl.ds(row, ROWS)], at(1, dt)
        )
    pl.semaphore_wait(reach.at[0], 2)
    for dz in (-4, 4):
        pl.semaphore_signal(reach.at[1], inc=1, device_id=at(0, 4 * dz), device_id_type=MESH)

    slot = lax.broadcasted_iota(jnp.int32, (LAYERS, 128), 1)

    def merge_columns(fields, rows):
        for r in rows:
            to_right, to_left = col_r[r], col_l[r]
            for f in range(fields):
                a = pltpu.roll(to_right, (128 - EDGE * f) % 128, 1)
                b = pltpu.roll(to_left, (256 - EDGE * (f + 1)) % 128, 1)
                rest = jnp.where(slot >= 128 - EDGE, b, 1.0 if f == CAP else 0.0)
                ext[f, r, :, COLS:] = jnp.where(slot < EDGE, a, rest)

    def make_couplings(rows, north, diagonals):
        for r in rows:
            east = ext[EAST, r]
            west = prev_col(east)
            south = ext[SOUTH, r]
            upward = ext[UP, r]
            downward = prev_layer(upward)
            d = ext[CAP, r] + east + west + south + north + upward + downward
            inv = 1.0 / d
            if diagonals:
                diag[0, r] = d
                diag[1, r] = inv
                g[0, r] = ext[LATE, r] * inv
            for i, c in enumerate((east, west, south, north, upward, downward)):
                coef[i, r] = c * inv
            north = south

    rows_near = range(HALO - NEAR, HALO + ROWS + NEAR)
    merge_columns(EARLY, rows_near)
    above = jnp.concatenate([sx[...], jnp.where(slot < 64, sx_r[...], sx_l[...])], axis=1)
    make_couplings(rows_near, above, True)

    def far_couplings():
        for c in halo[first:second]:
            c.wait_recv()
        end = HALO + ROWS + NEAR
        for rows in (range(0, HALO - NEAR), range(end, SPAN)):
            merge_columns(LATE, rows)
        make_couplings(range(1, HALO - NEAR), ext[SOUTH, 0], False)
        make_couplings(range(end, SPAN - 1), ext[SOUTH, end - 1], False)

    (q1, p1), (q2, p2), (q3, p3) = sweep_constants()

    def smooth(gi, ui, lo, hi):
        for r in range(lo + 1, hi - 1):
            z1[r] = ((1.0 + q1 - p1) / centre + p1) * gi[r] + (p1 / centre) * neighbours(gi, coef, r)
        for r in range(lo + 2, hi - 2):
            z2[r] = (1.0 + q2 - p2) * z1[r] + (p2 - q2 / centre) * gi[r] + p2 * neighbours(z1, coef, r)
        for r in range(lo + 3, hi - 3):
            ui[r] = (
                (1.0 + q3 - p3) * z2[r] - q3 * z1[r] + p3 * gi[r] + p3 * neighbours(z2, coef, r)
            )

    pending = []

    def send_all(src, targets, ssem, rsem):
        copies = []
        for n, (dt, dst) in enumerate(targets):
            c = pltpu.make_async_remote_copy(
                src_ref=src, dst_ref=dst, send_sem=ssem.at[n], recv_sem=rsem.at[n],
                device_id=at(0, dt), device_id_type=MESH,
            )
            c.start()
            copies.append(c)
        pending.extend(copies)
        return copies

    def send_u(i, n):
        return send_all(
            u.at[i, own], ((1, uh.at[n, pl.ds(0, NEAR)]), (-1, uh.at[n, pl.ds(NEAR, NEAR)])),
            ush_send.at[n], ush_recv.at[n],
        )

    def chain(base, beside):
        parts = [None] * 6
        spans = ((HALO - NEAR, HALO + ROWS + NEAR), (0, SPAN), (HALO - NEAR, HALO + ROWS + NEAR))
        for i, (lo, hi) in enumerate(spans):
            gi, ui = g.at[base + i], u.at[base + i]
            gn = g.at[base + i + 1] if i < 2 else z1
            smooth(gi, ui, lo, hi)
            for r in range(lo + 4, hi - 4):
                gn[r] = gi[r] - ui[r] + neighbours(ui, coef, r)
            if i == 0:
                k = base // 3
                copies = send_all(
                    gn.at[own],
                    [(dt, gn.at[pl.ds(row, ROWS)]) for dt, row in far + near],
                    mid_send.at[k], mid_recv.at[k],
                )
                beside()
            for r in range(HALO, HALO + ROWS):
                du = (diag[0, r] * ui[r])[:, :COLS]
                for k, ref in ((2 * i, gi), (2 * i + 1, gn)):
                    term = du * ref[r][:, :COLS]
                    parts[k] = term if parts[k] is None else parts[k] + term
            if i == 0:
                for c in copies:
                    c.wait_recv()
        lanes = lax.broadcasted_iota(jnp.int32, (1, 128), 1)
        row = jnp.zeros((1, 128), jnp.float32)
        for k, p in enumerate(parts):
            row = jnp.where(lanes == k, jnp.sum(p, axis=(0, 1), keepdims=True), row)
        return row

    def group_sum(buf, me, peers, n, ssem, rsem):
        for d in peers:
            pltpu.make_async_remote_copy(
                src_ref=buf.at[me], dst_ref=buf.at[me], send_sem=ssem, recv_sem=rsem,
                device_id=d, device_id_type=MESH,
            ).start()
        most = buf.at[pl.ds(0, n - 1)]
        whole = pltpu.make_async_remote_copy(
            src_ref=most, dst_ref=most, send_sem=ssem, recv_sem=rsem,
            device_id=peers[0], device_id_type=MESH,
        )
        whole.wait_recv()
        pending.append(whole)
        total = buf[0]
        for i in range(1, n):
            total = total + buf[i]
        return total

    def all_sum(bufs, base):
        c, p, w = bufs
        p[y * 4 + x] = group_sum(c, core, core_peer, 2, sum_send.at[base], sum_recv.at[base])
        w[z] = group_sum(p, y * 4 + x, plane_peers, 16, sum_send.at[base + 1], sum_recv.at[base + 1])
        return group_sum(w, z, z_peers, 16, sum_send.at[base + 2], sum_recv.at[base + 2])

    def coefficients(row):
        lanes = lax.broadcasted_iota(jnp.int32, (1, 128), 1)
        mu = [
            jnp.sum(jnp.where(lanes == k, row, 0.0), axis=(0, 1), keepdims=True) for k in range(6)
        ]
        return krylov_coefficients(mu)

    shadow = []

    def beside():
        shadow.extend(send_u(0, 0))
        far_couplings()

    a0[core] = chain(0, beside).reshape(1, 1, 128)
    shadow.extend(send_u(2, 1))
    for c in halo[second:]:
        c.wait_recv()
    for r in rows_near:
        ext[EARLY, r, :, COLS:] = jnp.where(slot < 64, early_r[r], early_l[r])
    for c in loads[8:10]:
        c.wait()
    pl.semaphore_wait(reach.at[1], 2)
    c1 = coefficients(all_sum((a0, a1, a2), 0).reshape(1, 128))
    for c in shadow:
        c.wait_recv()
    held = jnp.zeros((LAYERS, COLS), jnp.float32)
    for r in rows_near:
        inside = HALO <= r < HALO + ROWS
        if inside:
            ends = u[0, r], u[2, r]
        else:
            n = r - (HALO - NEAR) if r < HALO else r - HALO
            ends = uh[0, n], uh[1, n]
        v = c1[0] * ends[0] + c1[1] * u[1, r] + c1[2] * ends[1]
        g[3, r] = (ext[EARLY, r] + ext[CAP, r] * v) * diag[1, r]
        if inside:
            out_late[:, r - HALO, :] = v[:, :COLS]
            held = held + v[:, :COLS] * rate_late[:, r - HALO, :]

    stores = [
        pltpu.make_async_copy(src, dst, store_sem.at[n])
        for n, (src, dst) in enumerate(
            ((out_late, late_out), (out_early, early_out), (out_bank, bank_out))
        )
    ]
    stores[0].start()

    for c in loads[10:]:
        c.wait()
    moments = chain(3, lambda: None)
    terms = [held]
    for i in range(3):
        t = None
        for r in range(ROWS):
            w = u[3 + i, HALO + r][:, :COLS] * rate_early[:, r, :]
            t = w if t is None else t + w
        terms.append(t)

    hi = lax.Precision.HIGHEST
    f32 = jnp.float32

    def iota(shape, dim):
        return lax.broadcasted_iota(jnp.int32, shape, dim)

    spread = (iota((16, 128), 0) == iota((16, 128), 1) % 16).astype(f32)
    bank_of = jnp.dot(bank[...].astype(f32), spread, precision=hi, preferred_element_type=f32)
    mine = iota((LAYERS, 128), 0) == iota((LAYERS, 128), 1) // 16
    bank_row = jnp.sum(jnp.where(mine, bank_of, 0.0), axis=0, keepdims=True)
    chosen = (iota((BANKS, 128), 0) == (bank_row + 0.5).astype(jnp.int32)).astype(f32)
    tile_of = (iota((COLS, 128), 0) // DCOLS == iota((COLS, 128), 1) % 16).astype(f32)
    tiles = jnp.dot(jnp.concatenate(terms, axis=0), tile_of, precision=hi, preferred_element_type=f32)
    tiles = jnp.where(iota((4 * LAYERS, 128), 0) % LAYERS == iota((4 * LAYERS, 128), 1) // 16, tiles, 0.0)
    sums = lax.dot_general(
        tiles, chosen, (((1,), (1,)), ((), ())), precision=hi, preferred_element_type=f32
    )
    for i in range(4):
        s = jnp.sum(sums[i * LAYERS : (i + 1) * LAYERS], axis=0, keepdims=True)
        b0[core, 2 * i] = s[:, :128]
        b0[core, 2 * i + 1] = s[:, 128:]
    b0[core, 8] = moments

    total = all_sum((b0, b1, b2), 3)
    c2 = coefficients(total[8])
    for h in range(2):
        out_bank[:, h * 128 : (h + 1) * 128] = (
            total[h] + c2[0] * total[2 + h] + c2[1] * total[4 + h] + c2[2] * total[6 + h]
        )
    for r in range(ROWS):
        e = HALO + r
        v = c2[0] * u[3, e] + c2[1] * u[4, e] + c2[2] * u[5, e]
        out_early[:, r, :] = v[:, :COLS]
    stores[1].start()
    stores[2].start()
    for c in halo:
        c.wait_send()
    for c in pending:
        c.wait_send()
    for c in stores:
        c.wait()


def finish(late, early, bank, out_late, out_early, out_bank, late_v, early_v, bank_v, sem):
    ins = [
        pltpu.make_async_copy(src, dst, sem.at[n])
        for n, (src, dst) in enumerate(((late, late_v), (early, early_v), (bank, bank_v)))
    ]
    outs = [
        pltpu.make_async_copy(src, dst, sem.at[3 + n])
        for n, (src, dst) in enumerate(((late_v, out_late), (early_v, out_early), (bank_v, out_bank)))
    ]
    for c in ins:
        c.start()
    for c, d in zip(ins, outs):
        c.wait()
        d.start()
    for c in outs:
        c.wait()


def on_device(
    cond_x, cond_y, via_cond, capacity, class_map, via_mask, bank_map,
    source_late, source_early, rate_late, rate_early,
):
    f32, i32 = jnp.float32, jnp.int32
    hbm = pl.BlockSpec(memory_space=pltpu.HBM)
    dma = pltpu.SemaphoreType.DMA
    block = jax.ShapeDtypeStruct((LAYERS, ROWS, COLS), f32)
    shapes = (block, block, jax.ShapeDtypeStruct((1, BANKS), f32))
    wide = (SPAN, LAYERS, WIDE)
    field = pltpu.VMEM((LAYERS, ROWS, COLS), f32)
    results = pl.pallas_call(
        kernel,
        out_shape=shapes,
        in_specs=[hbm] * 11,
        out_specs=(hbm,) * 3,
        scratch_shapes=[
            field, field, pltpu.VMEM((1, BANKS), f32),
            field, field, field, field,
            pltpu.VMEM((ROWS, COLS), i32),
            pltpu.VMEM((LAYERS, NCLASS), i32),
            pltpu.VMEM((LAYERS, 16), i32),
            field, field, field, field,
            pltpu.VMEM((FIELDS,) + wide, f32),
            pltpu.VMEM((ROWS, LAYERS, 128), f32),
            pltpu.VMEM((ROWS, LAYERS, 128), f32),
            pltpu.VMEM((SPAN, LAYERS, 128), f32),
            pltpu.VMEM((SPAN, LAYERS, 128), f32),
            pltpu.VMEM((SPAN, LAYERS, 128), f32),
            pltpu.VMEM((SPAN, LAYERS, 128), f32),
            pltpu.VMEM((LAYERS, COLS), f32),
            pltpu.VMEM((LAYERS, 128), f32),
            pltpu.VMEM((LAYERS, 128), f32),
            pltpu.VMEM((6,) + wide, f32),
            pltpu.VMEM((2,) + wide, f32),
            pltpu.VMEM((6,) + wide, f32),
            pltpu.VMEM((6,) + wide, f32),
            pltpu.VMEM((2, 2 * NEAR, LAYERS, WIDE), f32),
            pltpu.VMEM(wide, f32),
            pltpu.VMEM(wide, f32),
            pltpu.VMEM((2, 1, 1, 128), f32),
            pltpu.VMEM((16, 1, 1, 128), f32),
            pltpu.VMEM((16, 1, 1, 128), f32),
            pltpu.VMEM((2, 9, 1, 128), f32),
            pltpu.VMEM((16, 9, 1, 128), f32),
            pltpu.VMEM((16, 9, 1, 128), f32),
            dma((11,)),
            dma((3,)),
            dma((25,)),
            dma((25,)),
            dma((2, 4)),
            dma((2, 4)),
            dma((2, 2)),
            dma((2, 2)),
            dma((6,)),
            dma((6,)),
            pltpu.SemaphoreType.REGULAR((2,)),
        ],
        compiler_params=pltpu.CompilerParams(
            collective_id=0, has_side_effects=True, vmem_limit_bytes=60 << 20
        ),
        name="adjoint_steps",
    )(
        cond_x, cond_y, via_cond, capacity, class_map, via_mask, bank_map.reshape(LAYERS, 16),
        source_late, source_early, rate_late, rate_early,
    )
    late, early, bank = pl.pallas_call(
        finish,
        out_shape=shapes,
        in_specs=[hbm] * 3,
        out_specs=(hbm,) * 3,
        scratch_shapes=[field, field, pltpu.VMEM((1, BANKS), f32), dma((6,))],
        compiler_params=pltpu.CompilerParams(vmem_limit_bytes=60 << 20),
        name="write_results",
    )(*results)
    return late, early, bank.reshape(BANKS)


def solution(mesh):
    block = P(None, "tile", "layer")
    in_specs = (block,) * 4 + (P("tile", "layer"), P()) + (block,) * 5
    return jax.shard_map(
        on_device, mesh=mesh, in_specs=in_specs, out_specs=(block, block, P()), check_vma=False
    )
```

```python
import functools

import jax
import jax.numpy as jnp
from jax import lax
from jax.experimental import pallas as pl
from jax.experimental.pallas import tpu as pltpu
from jax.sharding import PartitionSpec as P

MESH = pl.DeviceIdType.MESH
NCLASS = 8
DCOLS = 16
BANKS = 256
LAYERS = 8
ROWS = 4
COLS = 256
HALO = 4
SPAN = ROWS + 2 * HALO
WIDE = COLS + 128
EDGE = 24
FIELDS = 6
EAST, SOUTH, UP, CAP, LATE, EARLY = range(FIELDS)

lower_edge = 0.05
upper_edge = 2.0
centre = (lower_edge + upper_edge) / 2.0
half = (upper_edge - lower_edge) / 2.0
sigma = centre / half


def sweep_constants():
    out = []
    rho = 1.0 / sigma
    for _ in range(3):
        nxt = 1.0 / (2.0 * sigma - rho)
        out.append((nxt * rho, 2.0 * nxt / half))
        rho = nxt
    return out


def next_col(v):
    return pltpu.roll(v, WIDE - 1, 1)


def prev_col(v):
    return pltpu.roll(v, 1, 1)


def next_layer(v):
    return pltpu.roll(v, LAYERS - 1, 0)


def prev_layer(v):
    return pltpu.roll(v, 1, 0)


def neighbours(z, coef, r):
    v = z[r]
    acc = coef[0, r] * next_col(v) + coef[1, r] * prev_col(v)
    acc = acc + (coef[2, r] * z[r + 1] + coef[3, r] * z[r - 1])
    return acc + (coef[4, r] * next_layer(v) + coef[5, r] * prev_layer(v))


def krylov_coefficients(mu):
    zero = jnp.zeros_like(mu[0])
    one = zero + 1.0
    nu = [mu[s] - mu[s + 1] for s in range(5)]

    def form(c, moments):
        total = None
        for s in range(2 * len(c) - 1):
            w = None
            for i in range(len(c)):
                j = s - i
                if 0 <= j < len(c):
                    w = c[i] * c[j] if w is None else w + c[i] * c[j]
            total = w * moments[s] if total is None else total + w * moments[s]
        return total

    def plus(a, b, scale):
        n = max(len(a), len(b))
        a, b = a + [zero] * (n - len(a)), b + [zero] * (n - len(b))
        return [p + scale * q for p, q in zip(a, b)]

    res, sea, sol = [one], [one], []
    gamma = mu[0]
    for step in range(3):
        alpha = gamma / form(sea, nu)
        sol = plus(sol, sea, alpha)
        if step < 2:
            res = plus(plus(res, sea, -alpha), [zero] + sea, alpha)
            new = form(res, mu)
            sea = plus(res, sea, new / gamma)
            gamma = new
    return sol


def kernel(
    cond_x_in, cond_y_in, via_in, cap_in, cls_in, mask_in, bank_in, late_in, early_in, rate_late_in, rate_early_in,
    late_out, early_out, bank_out,
    out_late, out_early, out_bank, cond_x, cond_y, via, cap, cls, mask, bank, late, early, rate_late, rate_early,
    ext, pack_r, pack_l, col_r, col_l, early_r, early_l, sx, sx_r, sx_l, coef, diag, g, u, uh, pg, pu, pn, z1, z2,
    a0, a1, a2, b0, b1, b2,
    load_sem, store_sem, halo_send, halo_recv, mid_send, mid_recv, ush_send, ush_recv, sum_send, sum_recv, reach,
):
    loads = [
        pltpu.make_async_copy(src, dst, load_sem.at[n])
        for n, (src, dst) in enumerate((
            (cond_x_in, cond_x), (cond_y_in, cond_y), (via_in, via), (cap_in, cap), (cls_in, cls),
            (mask_in, mask), (late_in, late), (early_in, early), (bank_in, bank),
            (rate_late_in, rate_late), (rate_early_in, rate_early),
        ))
    ]
    for c in loads:
        c.start()

    lay = lax.axis_index("layer")
    til = lax.axis_index("tile")
    lays = lax.axis_size("layer")
    tils = lax.axis_size("tile")
    y, core = lay // 2, lay % 2
    z, x = til // 4, til % 4

    def at(dl, dt):
        return ((lay + dl + lays) % lays, (til + dt + tils) % tils)

    core_peer = [(lay + 1 - 2 * core, til)]
    plane_peers = [
        (((y + dy) % 4) * 2 + core, z * 4 + (x + dx) % 4)
        for dy in (2, 1, 3, 0) for dx in (2, 1, 3, 0) if (dy, dx) != (0, 0)
    ]
    z_peers = [
        (lay, ((z + i) % 16) * 4 + x) for i in sorted(range(1, 16), key=lambda i: -min(i, 16 - i))
    ]

    barrier = pltpu.get_barrier_semaphore()
    greet = [at(dl, dt) for dt in (-2, -1, 0, 1, 2) for dl in (-1, 0, 1) if (dl, dt) != (0, 0)]
    greet += plane_peers + [at(0, 4 * dz) for dz in (-2, 2, -1, 1)]
    for d in greet:
        pl.semaphore_signal(barrier, inc=1, device_id=d, device_id_type=MESH)

    lane = lax.broadcasted_iota(jnp.int32, (LAYERS, COLS), 1)
    layer = lax.broadcasted_iota(jnp.int32, (LAYERS, COLS), 0)
    last_col = jnp.logical_and(lane == COLS - 1, lay == lays - 1)
    top = layer == LAYERS - 1
    for c in loads[:8]:
        c.wait()
    masks = mask[...].astype(jnp.float32)
    for r in range(ROWS):
        e = HALO + r
        ext[EAST, e, :, :COLS] = jnp.where(last_col, 0.0, cond_x[:, r, :])
        south = cond_y[:, r, :]
        if r == ROWS - 1:
            south = jnp.where(til == tils - 1, 0.0, south)
        ext[SOUTH, e, :, :COLS] = south
        kind = jnp.broadcast_to(cls[r : r + 1, :], (LAYERS, COLS))
        opened = jnp.zeros((LAYERS, COLS), jnp.float32)
        for k in range(NCLASS):
            opened = jnp.where(kind == k, masks[:, k : k + 1], opened)
        ext[UP, e, :, :COLS] = jnp.where(top, 0.0, via[:, r, :] * opened)
        ext[CAP, e, :, :COLS] = cap[:, r, :]
        ext[LATE, e, :, :COLS] = late[:, r, :]
        ext[EARLY, e, :, :COLS] = early[:, r, :]
        lane128 = lax.broadcasted_iota(jnp.int32, (LAYERS, 128), 1)
        right = jnp.zeros((LAYERS, 128), jnp.float32)
        left = right
        for f in range(EARLY):
            here = jnp.logical_and(lane128 >= EDGE * f, lane128 < EDGE * (f + 1))
            v = ext[f, e, :, :128]
            right = jnp.where(here, pltpu.roll(v, EDGE * f, 1) if f else v, right)
            v = ext[f, e, :, COLS - 128 : COLS]
            left = jnp.where(here, pltpu.roll(v, (EDGE * (f + 1)) % 128, 1), left)
        pack_r[r] = right
        pack_l[r] = left

    pl.semaphore_wait(barrier, len(greet))
    for dz in (-2, 2):
        pl.semaphore_signal(reach.at[0], inc=1, device_id=at(0, 4 * dz), device_id_type=MESH)

    own = pl.ds(HALO, ROWS)
    halo = []

    def send(src, dst, peer):
        n = len(halo)
        halo.append(
            pltpu.make_async_remote_copy(
                src_ref=src, dst_ref=dst, send_sem=halo_send.at[n], recv_sem=halo_recv.at[n],
                device_id=peer, device_id_type=MESH,
            )
        )
        halo[-1].start()

    def send_rows(first, count, dt, row):
        fields = pl.ds(first, count)
        send(
            ext.at[fields, own, :, pl.ds(0, COLS)],
            ext.at[fields, pl.ds(row, ROWS), :, pl.ds(0, COLS)],
            at(0, dt),
        )

    def send_columns(dt, row):
        send(pack_r, col_r.at[pl.ds(row, ROWS)], at(-1, dt))
        send(pack_l, col_l.at[pl.ds(row, ROWS)], at(1, dt))

    near = ((1, 0), (-1, HALO + ROWS))
    last = ext.at[SOUTH, HALO + ROWS - 1]
    send(last.at[:, pl.ds(0, 128)], sx_r, at(-1, 2))
    send(last.at[:, pl.ds(COLS - 128, 128)], sx_l, at(1, 2))
    send(last.at[:, pl.ds(0, COLS)], sx, at(0, 2))
    for dt, row in near:
        send_columns(dt, row)
    for dt, row in near:
        send_rows(0, EARLY, dt, row)
    send_columns(0, HALO)
    first = len(halo)
    for c in halo:
        c.wait_recv()
    for dt, row in near + ((0, HALO),):
        if dt:
            send_rows(EARLY, 1, dt, row)
        send(ext.at[EARLY, own, :, pl.ds(0, 128)], early_r.at[pl.ds(row, ROWS)], at(-1, dt))
        send(
            ext.at[EARLY, own, :, pl.ds(COLS - 128, 128)], early_l.at[pl.ds(row, ROWS)], at(1, dt)
        )
    pl.semaphore_wait(reach.at[0], 2)
    for dz in (-4, 4):
        pl.semaphore_signal(reach.at[1], inc=1, device_id=at(0, 4 * dz), device_id_type=MESH)

    slot = lax.broadcasted_iota(jnp.int32, (LAYERS, 128), 1)

    for r in range(SPAN):
        to_right, to_left = col_r[r], col_l[r]
        for f in range(EARLY):
            a = pltpu.roll(to_right, (128 - EDGE * f) % 128, 1)
            b = pltpu.roll(to_left, (256 - EDGE * (f + 1)) % 128, 1)
            rest = jnp.where(slot >= 128 - EDGE, b, 1.0 if f == CAP else 0.0)
            ext[f, r, :, COLS:] = jnp.where(slot < EDGE, a, rest)
    north = jnp.concatenate([sx[...], jnp.where(slot < 64, sx_r[...], sx_l[...])], axis=1)
    for r in range(SPAN):
        east = ext[EAST, r]
        west = prev_col(east)
        south = ext[SOUTH, r]
        upward = ext[UP, r]
        downward = prev_layer(upward)
        d = ext[CAP, r] + east + west + south + north + upward + downward
        inv = 1.0 / d
        diag[0, r] = d
        diag[1, r] = inv
        g[0, r] = ext[LATE, r] * inv
        for i, c in enumerate((east, west, south, north, upward, downward)):
            coef[i, r] = c * inv
        north = south

    (q1, p1), (q2, p2), (q3, p3) = sweep_constants()

    def iterate(gi, ui, gn):
        for r in range(1, SPAN - 1):
            z1[r] = ((1.0 + q1 - p1) / centre + p1) * gi[r] + (p1 / centre) * neighbours(gi, coef, r)
        for r in range(2, SPAN - 2):
            z2[r] = (1.0 + q2 - p2) * z1[r] + (p2 - q2 / centre) * gi[r] + p2 * neighbours(z1, coef, r)
        for r in range(3, SPAN - 3):
            ui[r] = (
                (1.0 + q3 - p3) * z2[r] - q3 * z1[r] + p3 * gi[r] + p3 * neighbours(z2, coef, r)
            )
        for r in own_rows:
            gn[r] = gi[r] - ui[r] + neighbours(ui, coef, r)

    own_rows = range(HALO, HALO + ROWS)
    pending = []

    def send_block(src, above, below, ssem, rsem):
        copies = []
        for n, (dt, dst) in enumerate(((1, above), (-1, below))):
            c = pltpu.make_async_remote_copy(
                src_ref=src.at[own], dst_ref=dst, send_sem=ssem.at[n], recv_sem=rsem.at[n],
                device_id=at(0, dt), device_id_type=MESH,
            )
            c.start()
            copies.append(c)
        pending.extend(copies)
        return copies

    def send_g(ref, n):
        return send_block(
            ref, ref.at[pl.ds(0, HALO)], ref.at[pl.ds(HALO + ROWS, HALO)], mid_send.at[n], mid_recv.at[n]
        )

    def send_u(i):
        return send_block(
            u.at[i], uh.at[i, pl.ds(0, HALO)], uh.at[i, pl.ds(HALO, HALO)],
            ush_send.at[i], ush_recv.at[i],
        )

    def arrive(copies):
        for c in copies:
            c.wait_recv()

    def add_products(parts, i, gi, ui, gn):
        for r in own_rows:
            du = (diag[0, r] * ui[r])[:, :COLS]
            for k, ref in ((2 * i, gi), (2 * i + 1, gn)):
                term = du * ref[r][:, :COLS]
                parts[k] = term if parts[k] is None else parts[k] + term

    def moment_row(parts):
        lanes = lax.broadcasted_iota(jnp.int32, (1, 128), 1)
        row = jnp.zeros((1, 128), jnp.float32)
        for k, p in enumerate(parts):
            row = jnp.where(lanes == k, jnp.sum(p, axis=(0, 1), keepdims=True), row)
        return row

    def group_sum(buf, me, peers, n, ssem, rsem, beside=None):
        for d in peers:
            pltpu.make_async_remote_copy(
                src_ref=buf.at[me], dst_ref=buf.at[me], send_sem=ssem, recv_sem=rsem,
                device_id=d, device_id_type=MESH,
            ).start()
        most = buf.at[pl.ds(0, n - 1)]
        whole = pltpu.make_async_remote_copy(
            src_ref=most, dst_ref=most, send_sem=ssem, recv_sem=rsem,
            device_id=peers[0], device_id_type=MESH,
        )
        if beside is not None:
            beside()
        whole.wait_recv()
        pending.append(whole)
        total = buf[0]
        for i in range(1, n):
            total = total + buf[i]
        return total

    def all_sum(bufs, base, beside=(None, None, None)):
        c, p, w = bufs
        xy = y * 4 + x
        send, recv = sum_send.at, sum_recv.at
        p[xy] = group_sum(c, core, core_peer, 2, send[base], recv[base], beside[0])
        w[z] = group_sum(p, xy, plane_peers, 16, send[base + 1], recv[base + 1], beside[1])
        return group_sum(w, z, z_peers, 16, send[base + 2], recv[base + 2], beside[2])

    def coefficients(row):
        lanes = lax.broadcasted_iota(jnp.int32, (1, 128), 1)
        mu = [
            jnp.sum(jnp.where(lanes == k, row, 0.0), axis=(0, 1), keepdims=True) for k in range(6)
        ]
        return krylov_coefficients(mu)

    parts = [None] * 6
    iterate(g.at[0], u.at[0], g.at[1])
    moving = send_g(g.at[1], 0)
    shared = [send_u(0)]
    add_products(parts, 0, g.at[0], u.at[0], g.at[1])
    arrive(moving)
    iterate(g.at[1], u.at[1], g.at[2])
    moving = send_g(g.at[2], 1)
    shared.append(send_u(1))
    add_products(parts, 1, g.at[1], u.at[1], g.at[2])
    traded = []

    def source_part():
        arrive(halo[first:])
        for r in range(SPAN):
            ext[EARLY, r, :, COLS:] = jnp.where(slot < 64, early_r[r], early_l[r])
            pg[0, r] = ext[EARLY, r] * diag[1, r]
        iterate(pg.at[0], pu.at[0], pn.at[0])
        traded.extend(send_g(pn.at[0], 2))

    def field_part(i):
        arrive(shared[i])
        for r in range(SPAN):
            if r in own_rows:
                v = u[i, r]
            else:
                v = uh[i, r if r < HALO else r - ROWS]
            pg[1 + i, r] = ext[CAP, r] * diag[1, r] * v
        iterate(pg.at[1 + i], pu.at[1 + i], pn.at[1 + i])
        traded.extend(send_g(pn.at[1 + i], 3 + i))

    source_part()
    field_part(0)
    arrive(moving)
    iterate(g.at[2], u.at[2], z1)
    add_products(parts, 2, g.at[2], u.at[2], z1)
    a0[core] = moment_row(parts).reshape(1, 1, 128)
    for c in loads[8:10]:
        c.wait()
    pl.semaphore_wait(reach.at[1], 2)
    row = all_sum(
        (a0, a1, a2), 0,
        (lambda: shared.append(send_u(2)), lambda: field_part(1), lambda: field_part(2)),
    )
    c1 = coefficients(row.reshape(1, 128))
    arrive(traded)
    held = jnp.zeros((LAYERS, COLS), jnp.float32)
    for r in range(SPAN):
        g[3, r] = pn[0, r] + c1[0] * pn[1, r] + c1[1] * pn[2, r] + c1[2] * pn[3, r]
        if r in own_rows:
            g[5, r] = pg[0, r] + c1[0] * pg[1, r] + c1[1] * pg[2, r] + c1[2] * pg[3, r]
            u[5, r] = pu[0, r] + c1[0] * pu[1, r] + c1[1] * pu[2, r] + c1[2] * pu[3, r]
    parts = [None] * 6
    iterate(g.at[3], u.at[3], g.at[4])
    moving = send_g(g.at[4], 6)
    for r in own_rows:
        v = c1[0] * u[0, r] + c1[1] * u[1, r] + c1[2] * u[2, r]
        out_late[:, r - HALO, :] = v[:, :COLS]
        held = held + v[:, :COLS] * rate_late[:, r - HALO, :]
    stores = [
        pltpu.make_async_copy(src, dst, store_sem.at[n])
        for n, (src, dst) in enumerate(
            ((out_late, late_out), (out_early, early_out), (out_bank, bank_out))
        )
    ]
    stores[0].start()

    add_products(parts, 0, g.at[5], u.at[5], g.at[3])
    add_products(parts, 1, g.at[3], u.at[3], g.at[4])
    for c in loads[10:]:
        c.wait()
    arrive(moving)
    iterate(g.at[4], u.at[4], z1)
    add_products(parts, 2, g.at[4], u.at[4], z1)
    moments = moment_row(parts)
    terms = [held]
    for i in (5, 3, 4):
        t = None
        for r in own_rows:
            w = u[i, r][:, :COLS] * rate_early[:, r - HALO, :]
            t = w if t is None else t + w
        terms.append(t)

    hi = lax.Precision.HIGHEST
    f32 = jnp.float32

    def iota(shape, dim):
        return lax.broadcasted_iota(jnp.int32, shape, dim)

    spread = (iota((16, 128), 0) == iota((16, 128), 1) % 16).astype(f32)
    bank_of = jnp.dot(bank[...].astype(f32), spread, precision=hi, preferred_element_type=f32)
    mine = iota((LAYERS, 128), 0) == iota((LAYERS, 128), 1) // 16
    bank_row = jnp.sum(jnp.where(mine, bank_of, 0.0), axis=0, keepdims=True)
    chosen = (iota((BANKS, 128), 0) == (bank_row + 0.5).astype(jnp.int32)).astype(f32)
    tile_of = (iota((COLS, 128), 0) // DCOLS == iota((COLS, 128), 1) % 16).astype(f32)
    tiles = jnp.dot(jnp.concatenate(terms, axis=0), tile_of, precision=hi, preferred_element_type=f32)
    tiles = jnp.where(iota((4 * LAYERS, 128), 0) % LAYERS == iota((4 * LAYERS, 128), 1) // 16, tiles, 0.0)
    sums = lax.dot_general(
        tiles, chosen, (((1,), (1,)), ((), ())), precision=hi, preferred_element_type=f32
    )
    for i in range(4):
        s = jnp.sum(sums[i * LAYERS : (i + 1) * LAYERS], axis=0, keepdims=True)
        b0[core, 2 * i] = s[:, :128]
        b0[core, 2 * i + 1] = s[:, 128:]
    b0[core, 8] = moments

    total = all_sum((b0, b1, b2), 3)
    c2 = coefficients(total[8])
    for h in range(2):
        out_bank[:, h * 128 : (h + 1) * 128] = (
            total[h] + c2[0] * total[2 + h] + c2[1] * total[4 + h] + c2[2] * total[6 + h]
        )
    for r in range(ROWS):
        e = HALO + r
        v = c2[0] * u[5, e] + c2[1] * u[3, e] + c2[2] * u[4, e]
        out_early[:, r, :] = v[:, :COLS]
    stores[1].start()
    stores[2].start()
    for c in halo:
        c.wait_send()
    for c in pending:
        c.wait_send()
    for c in stores:
        c.wait()


def finish(late, early, bank, out_late, out_early, out_bank, late_v, early_v, bank_v, sem):
    ins = [
        pltpu.make_async_copy(src, dst, sem.at[n])
        for n, (src, dst) in enumerate(((late, late_v), (early, early_v), (bank, bank_v)))
    ]
    outs = [
        pltpu.make_async_copy(src, dst, sem.at[3 + n])
        for n, (src, dst) in enumerate(((late_v, out_late), (early_v, out_early), (bank_v, out_bank)))
    ]
    for c in ins:
        c.start()
    for c, d in zip(ins, outs):
        c.wait()
        d.start()
    for c in outs:
        c.wait()


def on_device(
    cond_x, cond_y, via_cond, capacity, class_map, via_mask, bank_map,
    source_late, source_early, rate_late, rate_early,
):
    f32, i32 = jnp.float32, jnp.int32
    hbm = pl.BlockSpec(memory_space=pltpu.HBM)
    dma = pltpu.SemaphoreType.DMA
    block = jax.ShapeDtypeStruct((LAYERS, ROWS, COLS), f32)
    shapes = (block, block, jax.ShapeDtypeStruct((1, BANKS), f32))
    wide = (SPAN, LAYERS, WIDE)
    field = pltpu.VMEM((LAYERS, ROWS, COLS), f32)
    results = pl.pallas_call(
        kernel,
        out_shape=shapes,
        in_specs=[hbm] * 11,
        out_specs=(hbm,) * 3,
        scratch_shapes=[
            field, field, pltpu.VMEM((1, BANKS), f32),
            field, field, field, field,
            pltpu.VMEM((ROWS, COLS), i32),
            pltpu.VMEM((LAYERS, NCLASS), i32),
            pltpu.VMEM((LAYERS, 16), i32),
            field, field, field, field,
            pltpu.VMEM((FIELDS,) + wide, f32),
            pltpu.VMEM((ROWS, LAYERS, 128), f32),
            pltpu.VMEM((ROWS, LAYERS, 128), f32),
            pltpu.VMEM((SPAN, LAYERS, 128), f32),
            pltpu.VMEM((SPAN, LAYERS, 128), f32),
            pltpu.VMEM((SPAN, LAYERS, 128), f32),
            pltpu.VMEM((SPAN, LAYERS, 128), f32),
            pltpu.VMEM((LAYERS, COLS), f32),
            pltpu.VMEM((LAYERS, 128), f32),
            pltpu.VMEM((LAYERS, 128), f32),
            pltpu.VMEM((6,) + wide, f32),
            pltpu.VMEM((2,) + wide, f32),
            pltpu.VMEM((6,) + wide, f32),
            pltpu.VMEM((6,) + wide, f32),
            pltpu.VMEM((3, 2 * HALO, LAYERS, WIDE), f32),
            pltpu.VMEM((4,) + wide, f32),
            pltpu.VMEM((4,) + wide, f32),
            pltpu.VMEM((4,) + wide, f32),
            pltpu.VMEM(wide, f32),
            pltpu.VMEM(wide, f32),
            pltpu.VMEM((2, 1, 1, 128), f32),
            pltpu.VMEM((16, 1, 1, 128), f32),
            pltpu.VMEM((16, 1, 1, 128), f32),
            pltpu.VMEM((2, 9, 1, 128), f32),
            pltpu.VMEM((16, 9, 1, 128), f32),
            pltpu.VMEM((16, 9, 1, 128), f32),
            dma((11,)),
            dma((3,)),
            dma((19,)),
            dma((19,)),
            dma((7, 2)),
            dma((7, 2)),
            dma((3, 2)),
            dma((3, 2)),
            dma((6,)),
            dma((6,)),
            pltpu.SemaphoreType.REGULAR((2,)),
        ],
        compiler_params=pltpu.CompilerParams(
            collective_id=0, has_side_effects=True, vmem_limit_bytes=60 << 20
        ),
        name="adjoint_steps",
    )(
        cond_x, cond_y, via_cond, capacity, class_map, via_mask, bank_map.reshape(LAYERS, 16),
        source_late, source_early, rate_late, rate_early,
    )
    late, early, bank = pl.pallas_call(
        finish,
        out_shape=shapes,
        in_specs=[hbm] * 3,
        out_specs=(hbm,) * 3,
        scratch_shapes=[field, field, pltpu.VMEM((1, BANKS), f32), dma((6,))],
        compiler_params=pltpu.CompilerParams(vmem_limit_bytes=60 << 20),
        name="write_results",
    )(*results)
    return late, early, bank.reshape(BANKS)


def solution(mesh):
    block = P(None, "tile", "layer")
    in_specs = (block,) * 4 + (P("tile", "layer"), P()) + (block,) * 5
    return jax.shard_map(
        on_device, mesh=mesh, in_specs=in_specs, out_specs=(block, block, P()), check_vma=False
    )
```

```python
import functools

import jax
import jax.numpy as jnp
from jax import lax
from jax.experimental import pallas as pl
from jax.experimental.pallas import tpu as pltpu
from jax.sharding import PartitionSpec as P

MESH = pl.DeviceIdType.MESH
NCLASS = 8
DCOLS = 16
BANKS = 256
LAYERS = 8
ROWS = 4
COLS = 256
HALO = 4
SPAN = ROWS + 2 * HALO
WIDE = COLS + 128
EDGE = 24
FIELDS = 6
EAST, SOUTH, UP, CAP, LATE, EARLY = range(FIELDS)

lower_edge = 0.05
upper_edge = 2.0
centre = (lower_edge + upper_edge) / 2.0
half = (upper_edge - lower_edge) / 2.0
sigma = centre / half


def sweep_constants():
    out = []
    rho = 1.0 / sigma
    for _ in range(3):
        nxt = 1.0 / (2.0 * sigma - rho)
        out.append((nxt * rho, 2.0 * nxt / half))
        rho = nxt
    return out


def next_col(v):
    return pltpu.roll(v, WIDE - 1, 1)


def prev_col(v):
    return pltpu.roll(v, 1, 1)


def next_layer(v):
    return pltpu.roll(v, LAYERS - 1, 0)


def prev_layer(v):
    return pltpu.roll(v, 1, 0)


def neighbours(z, coef, r):
    v = z[r]
    acc = coef[0, r] * next_col(v) + coef[1, r] * prev_col(v)
    acc = acc + (coef[2, r] * z[r + 1] + coef[3, r] * z[r - 1])
    return acc + (coef[4, r] * next_layer(v) + coef[5, r] * prev_layer(v))


def krylov_coefficients(mu):
    zero = jnp.zeros_like(mu[0])
    one = zero + 1.0
    nu = [mu[s] - mu[s + 1] for s in range(5)]

    def form(c, moments):
        total = None
        for s in range(2 * len(c) - 1):
            w = None
            for i in range(len(c)):
                j = s - i
                if 0 <= j < len(c):
                    w = c[i] * c[j] if w is None else w + c[i] * c[j]
            total = w * moments[s] if total is None else total + w * moments[s]
        return total

    def plus(a, b, scale):
        n = max(len(a), len(b))
        a, b = a + [zero] * (n - len(a)), b + [zero] * (n - len(b))
        return [p + scale * q for p, q in zip(a, b)]

    res, sea, sol = [one], [one], []
    gamma = mu[0]
    for step in range(3):
        alpha = gamma / form(sea, nu)
        sol = plus(sol, sea, alpha)
        if step < 2:
            res = plus(plus(res, sea, -alpha), [zero] + sea, alpha)
            new = form(res, mu)
            sea = plus(res, sea, new / gamma)
            gamma = new
    return sol


def kernel(
    cond_x_in, cond_y_in, via_in, cap_in, cls_in, mask_in, bank_in, late_in, early_in, rate_late_in, rate_early_in,
    late_out, early_out, bank_out,
    out_late, out_early, out_bank, cond_x, cond_y, via, cap, cls, mask, bank, late, early, rate_late, rate_early,
    ext, pack_r, pack_l, col_r, col_l, early_r, early_l, sx, sx_r, sx_l, coef, diag, g, u, uh, pg, pu, z1, z2,
    a0, a1, a2, b0, b1, b2, b3,
    load_sem, store_sem, halo_send, halo_recv, mid_send, mid_recv, ush_send, ush_recv, sum_send, sum_recv, reach,
):
    loads = [
        pltpu.make_async_copy(src, dst, load_sem.at[n])
        for n, (src, dst) in enumerate((
            (cond_x_in, cond_x), (cond_y_in, cond_y), (via_in, via), (cap_in, cap), (cls_in, cls),
            (mask_in, mask), (late_in, late), (early_in, early), (bank_in, bank),
            (rate_late_in, rate_late), (rate_early_in, rate_early),
        ))
    ]
    for c in loads:
        c.start()

    lay = lax.axis_index("layer")
    til = lax.axis_index("tile")
    lays = lax.axis_size("layer")
    tils = lax.axis_size("tile")
    y, core = lay // 2, lay % 2
    z, x = til // 4, til % 4

    around = {
        (dl, dt): ((lay + dl + lays) % lays, (til + dt + tils) % tils)
        for dt in (-16, -8, -4, -2, -1, 0, 1, 2, 4, 8, 16)
        for dl in ((-1, 0, 1) if -2 <= dt <= 2 else (0,))
    }

    def at(dl, dt):
        return around[dl, dt]

    core_peer = [(lay + 1 - 2 * core, til)]
    plane_peers = [
        (((y + dy) % 4) * 2 + core, z * 4 + (x + dx) % 4)
        for dy in (2, 1, 3, 0) for dx in (2, 1, 3, 0) if (dy, dx) != (0, 0)
    ]
    z_peers = [
        (lay, ((z + i) % 16) * 4 + x) for i in sorted(range(1, 16), key=lambda i: -min(i, 16 - i))
    ]

    barrier = pltpu.get_barrier_semaphore()
    greet = [at(dl, dt) for dt in (-2, -1, 0, 1, 2) for dl in (-1, 0, 1) if (dl, dt) != (0, 0)]
    greet += plane_peers + [at(0, 4 * dz) for dz in (-2, 2, -1, 1)]
    for d in greet:
        pl.semaphore_signal(barrier, inc=1, device_id=d, device_id_type=MESH)

    lane = lax.broadcasted_iota(jnp.int32, (LAYERS, COLS), 1)
    layer = lax.broadcasted_iota(jnp.int32, (LAYERS, COLS), 0)
    last_col = jnp.logical_and(lane == COLS - 1, lay == lays - 1)
    top = layer == LAYERS - 1
    for c in loads[:8]:
        c.wait()
    masks = mask[...].astype(jnp.float32)
    for r in range(ROWS):
        e = HALO + r
        ext[EAST, e, :, :COLS] = jnp.where(last_col, 0.0, cond_x[:, r, :])
        south = cond_y[:, r, :]
        if r == ROWS - 1:
            south = jnp.where(til == tils - 1, 0.0, south)
        ext[SOUTH, e, :, :COLS] = south
        kind = jnp.broadcast_to(cls[r : r + 1, :], (LAYERS, COLS))
        opened = jnp.zeros((LAYERS, COLS), jnp.float32)
        for k in range(NCLASS):
            opened = jnp.where(kind == k, masks[:, k : k + 1], opened)
        ext[UP, e, :, :COLS] = jnp.where(top, 0.0, via[:, r, :] * opened)
        ext[CAP, e, :, :COLS] = cap[:, r, :]
        ext[LATE, e, :, :COLS] = late[:, r, :]
        ext[EARLY, e, :, :COLS] = early[:, r, :]
        lane128 = lax.broadcasted_iota(jnp.int32, (LAYERS, 128), 1)
        right = jnp.zeros((LAYERS, 128), jnp.float32)
        left = right
        for f in range(EARLY):
            here = jnp.logical_and(lane128 >= EDGE * f, lane128 < EDGE * (f + 1))
            v = ext[f, e, :, :128]
            right = jnp.where(here, pltpu.roll(v, EDGE * f, 1) if f else v, right)
            v = ext[f, e, :, COLS - 128 : COLS]
            left = jnp.where(here, pltpu.roll(v, (EDGE * (f + 1)) % 128, 1), left)
        pack_r[r] = right
        pack_l[r] = left

    pl.semaphore_wait(barrier, len(greet))
    for dz in (-2, 2):
        pl.semaphore_signal(reach.at[0], inc=1, device_id=at(0, 4 * dz), device_id_type=MESH)

    own = pl.ds(HALO, ROWS)
    halo = []

    def send(src, dst, peer):
        n = len(halo)
        halo.append(
            pltpu.make_async_remote_copy(
                src_ref=src, dst_ref=dst, send_sem=halo_send.at[n], recv_sem=halo_recv.at[n],
                device_id=peer, device_id_type=MESH,
            )
        )
        halo[-1].start()

    def send_rows(first, count, dt, row):
        fields = pl.ds(first, count)
        send(
            ext.at[fields, own, :, pl.ds(0, COLS)],
            ext.at[fields, pl.ds(row, ROWS), :, pl.ds(0, COLS)],
            at(0, dt),
        )

    def send_columns(dt, row):
        send(pack_r, col_r.at[pl.ds(row, ROWS)], at(-1, dt))
        send(pack_l, col_l.at[pl.ds(row, ROWS)], at(1, dt))

    near = ((1, 0), (-1, HALO + ROWS))
    last = ext.at[SOUTH, HALO + ROWS - 1]
    send(last.at[:, pl.ds(0, 128)], sx_r, at(-1, 2))
    send(last.at[:, pl.ds(COLS - 128, 128)], sx_l, at(1, 2))
    send(last.at[:, pl.ds(0, COLS)], sx, at(0, 2))
    for dt, row in near:
        send_columns(dt, row)
    for dt, row in near:
        send_rows(0, EARLY, dt, row)
    send_columns(0, HALO)
    first = len(halo)
    for c in halo:
        c.wait_recv()
    for dt, row in near + ((0, HALO),):
        if dt:
            send_rows(EARLY, 1, dt, row)
        send(ext.at[EARLY, own, :, pl.ds(0, 128)], early_r.at[pl.ds(row, ROWS)], at(-1, dt))
        send(
            ext.at[EARLY, own, :, pl.ds(COLS - 128, 128)], early_l.at[pl.ds(row, ROWS)], at(1, dt)
        )
    pl.semaphore_wait(reach.at[0], 2)
    for dz in (-4, 4):
        pl.semaphore_signal(reach.at[1], inc=1, device_id=at(0, 4 * dz), device_id_type=MESH)

    slot = lax.broadcasted_iota(jnp.int32, (LAYERS, 128), 1)

    for r in range(SPAN):
        to_right, to_left = col_r[r], col_l[r]
        for f in range(EARLY):
            a = pltpu.roll(to_right, (128 - EDGE * f) % 128, 1)
            b = pltpu.roll(to_left, (256 - EDGE * (f + 1)) % 128, 1)
            rest = jnp.where(slot >= 128 - EDGE, b, 1.0 if f == CAP else 0.0)
            ext[f, r, :, COLS:] = jnp.where(slot < EDGE, a, rest)
    north = jnp.concatenate([sx[...], jnp.where(slot < 64, sx_r[...], sx_l[...])], axis=1)
    for r in range(SPAN):
        east = ext[EAST, r]
        west = prev_col(east)
        south = ext[SOUTH, r]
        upward = ext[UP, r]
        downward = prev_layer(upward)
        d = ext[CAP, r] + east + west + south + north + upward + downward
        inv = 1.0 / d
        diag[0, r] = d
        diag[1, r] = inv
        g[0, r] = ext[LATE, r] * inv
        for i, c in enumerate((east, west, south, north, upward, downward)):
            coef[i, r] = c * inv
        north = south

    (q1, p1), (q2, p2), (q3, p3) = sweep_constants()

    def iterate(gi, ui, gn):
        for r in range(1, SPAN - 1):
            z1[r] = ((1.0 + q1 - p1) / centre + p1) * gi[r] + (p1 / centre) * neighbours(gi, coef, r)
        for r in range(2, SPAN - 2):
            z2[r] = (1.0 + q2 - p2) * z1[r] + (p2 - q2 / centre) * gi[r] + p2 * neighbours(z1, coef, r)
        for r in range(3, SPAN - 3):
            ui[r] = (
                (1.0 + q3 - p3) * z2[r] - q3 * z1[r] + p3 * gi[r] + p3 * neighbours(z2, coef, r)
            )
        for r in own_rows:
            gn[r] = gi[r] - ui[r] + neighbours(ui, coef, r)

    own_rows = range(HALO, HALO + ROWS)
    pending = []

    def send_block(src, above, below, ssem, rsem):
        copies = []
        for n, (dt, dst) in enumerate(((1, above), (-1, below))):
            c = pltpu.make_async_remote_copy(
                src_ref=src.at[own], dst_ref=dst, send_sem=ssem.at[n], recv_sem=rsem.at[n],
                device_id=at(0, dt), device_id_type=MESH,
            )
            c.start()
            copies.append(c)
        pending.extend(copies)
        return copies

    def send_g(ref, n):
        return send_block(
            ref, ref.at[pl.ds(0, HALO)], ref.at[pl.ds(HALO + ROWS, HALO)], mid_send.at[n], mid_recv.at[n]
        )

    def send_u(i):
        return send_block(
            u.at[i], uh.at[i, pl.ds(0, HALO)], uh.at[i, pl.ds(HALO, HALO)],
            ush_send.at[i], ush_recv.at[i],
        )

    def arrive(copies):
        for c in copies:
            c.wait_recv()

    def add_products(parts, i, gi, ui, gn):
        for r in own_rows:
            du = (diag[0, r] * ui[r])[:, :COLS]
            for k, ref in ((2 * i, gi), (2 * i + 1, gn)):
                term = du * ref[r][:, :COLS]
                parts[k] = term if parts[k] is None else parts[k] + term

    def moment_row(parts):
        lanes = lax.broadcasted_iota(jnp.int32, (1, 128), 1)
        row = jnp.zeros((1, 128), jnp.float32)
        for k, p in enumerate(parts):
            row = jnp.where(lanes == k, jnp.sum(p, axis=(0, 1), keepdims=True), row)
        return row

    def group_sum(buf, me, peers, n, ssem, rsem, beside=None):
        for d in peers:
            pltpu.make_async_remote_copy(
                src_ref=buf.at[me], dst_ref=buf.at[me], send_sem=ssem, recv_sem=rsem,
                device_id=d, device_id_type=MESH,
            ).start()
        most = buf.at[pl.ds(0, n - 1)]
        whole = pltpu.make_async_remote_copy(
            src_ref=most, dst_ref=most, send_sem=ssem, recv_sem=rsem,
            device_id=peers[0], device_id_type=MESH,
        )
        if beside is not None:
            beside()
        whole.wait_recv()
        pending.append(whole)
        total = buf[0]
        for i in range(1, n):
            total = total + buf[i]
        return total

    def all_sum(bufs, base, beside=(None, None, None)):
        c, p, w = bufs
        xy = y * 4 + x
        send, recv = sum_send.at, sum_recv.at
        p[xy] = group_sum(c, core, core_peer, 2, send[base], recv[base], beside[0])
        w[z] = group_sum(p, xy, plane_peers, 16, send[base + 1], recv[base + 1], beside[1])
        return group_sum(w, z, z_peers, 16, send[base + 2], recv[base + 2], beside[2])

    def coefficients(row):
        lanes = lax.broadcasted_iota(jnp.int32, (1, 128), 1)
        mu = [
            jnp.sum(jnp.where(lanes == k, row, 0.0), axis=(0, 1), keepdims=True) for k in range(6)
        ]
        return krylov_coefficients(mu)

    parts = [None] * 6
    iterate(g.at[0], u.at[0], g.at[1])
    moving = send_g(g.at[1], 0)
    shared = [send_u(0)]
    add_products(parts, 0, g.at[0], u.at[0], g.at[1])
    arrive(moving)
    iterate(g.at[1], u.at[1], g.at[2])
    moving = send_g(g.at[2], 1)
    shared.append(send_u(1))
    add_products(parts, 1, g.at[1], u.at[1], g.at[2])
    traded = {}

    def part_step(step, n):
        if step:
            arrive(traded[0, n])
        iterate(pg.at[step, n], pu.at[step, n], pg.at[step + 1, n])
        traded[step, n] = send_g(pg.at[step + 1, n], 2 + 4 * step + n)

    def source_part():
        arrive(halo[first:])
        for r in range(SPAN):
            ext[EARLY, r, :, COLS:] = jnp.where(slot < 64, early_r[r], early_l[r])
            pg[0, 0, r] = ext[EARLY, r] * diag[1, r]
        part_step(0, 0)

    def field_part(i):
        arrive(shared[i])
        for r in range(SPAN):
            if r in own_rows:
                v = u[i, r]
            else:
                v = uh[i, r if r < HALO else r - ROWS]
            pg[0, 1 + i, r] = ext[CAP, r] * diag[1, r] * v
        part_step(0, 1 + i)

    source_part()
    field_part(0)
    arrive(moving)
    iterate(g.at[2], u.at[2], z1)
    shared.append(send_u(2))
    add_products(parts, 2, g.at[2], u.at[2], z1)
    a0[core] = moment_row(parts).reshape(1, 1, 128)
    for c in loads[8:10]:
        c.wait()
    pl.semaphore_wait(reach.at[1], 2)

    def beside_plane():
        field_part(1)
        field_part(2)

    def beside_z():
        for n in (0, 1, 2, 3):
            part_step(1, n)

    row = all_sum((a0, a1, a2), 0, (None, beside_plane, beside_z))
    c1 = coefficients(row.reshape(1, 128))

    def added(ref, r):
        return ref[0, r] + c1[0] * ref[1, r] + c1[1] * ref[2, r] + c1[2] * ref[3, r]

    for n in range(4):
        arrive(traded[1, n])
    for r in range(SPAN):
        g[5, r] = added(pg.at[2], r)
    iterate(g.at[5], u.at[5], z1)
    held = jnp.zeros((LAYERS, COLS), jnp.float32)
    for r in own_rows:
        g[3, r] = added(pg.at[0], r)
        g[4, r] = added(pg.at[1], r)
        u[3, r] = added(pu.at[0], r)
        u[4, r] = added(pu.at[1], r)
        v = c1[0] * u[0, r] + c1[1] * u[1, r] + c1[2] * u[2, r]
        out_late[:, r - HALO, :] = v[:, :COLS]
        held = held + v[:, :COLS] * rate_late[:, r - HALO, :]
    stores = [
        pltpu.make_async_copy(src, dst, store_sem.at[n])
        for n, (src, dst) in enumerate(
            ((out_late, late_out), (out_early, early_out), (out_bank, bank_out))
        )
    ]
    stores[0].start()

    parts = [None] * 6
    add_products(parts, 0, g.at[3], u.at[3], g.at[4])
    add_products(parts, 1, g.at[4], u.at[4], g.at[5])
    add_products(parts, 2, g.at[5], u.at[5], z1)
    for c in loads[10:]:
        c.wait()
    moments = moment_row(parts)
    terms = [held]
    for i in (3, 4, 5):
        t = None
        for r in own_rows:
            w = u[i, r][:, :COLS] * rate_early[:, r - HALO, :]
            t = w if t is None else t + w
        terms.append(t)

    hi = lax.Precision.HIGHEST
    f32 = jnp.float32

    def iota(shape, dim):
        return lax.broadcasted_iota(jnp.int32, shape, dim)

    spread = (iota((16, 128), 0) == iota((16, 128), 1) % 16).astype(f32)
    bank_of = jnp.dot(bank[...].astype(f32), spread, precision=hi, preferred_element_type=f32)
    mine = iota((LAYERS, 128), 0) == iota((LAYERS, 128), 1) // 16
    bank_row = jnp.sum(jnp.where(mine, bank_of, 0.0), axis=0, keepdims=True)
    chosen = (iota((BANKS, 128), 0) == (bank_row + 0.5).astype(jnp.int32)).astype(f32)
    tile_of = (iota((COLS, 128), 0) // DCOLS == iota((COLS, 128), 1) % 16).astype(f32)
    tiles = jnp.dot(jnp.concatenate(terms, axis=0), tile_of, precision=hi, preferred_element_type=f32)
    tiles = jnp.where(iota((4 * LAYERS, 128), 0) % LAYERS == iota((4 * LAYERS, 128), 1) // 16, tiles, 0.0)
    sums = lax.dot_general(
        tiles, chosen, (((1,), (1,)), ((), ())), precision=hi, preferred_element_type=f32
    )
    b0[core, 0] = moments
    for i in range(4):
        s = jnp.sum(sums[i * LAYERS : (i + 1) * LAYERS], axis=0, keepdims=True)
        b0[core, 1 + 2 * i] = s[:, :128]
        b0[core, 2 + 2 * i] = s[:, 128:]

    both = group_sum(b0, core, core_peer, 2, sum_send.at[3], sum_recv.at[3])
    xy = y * 4 + x
    b1[xy, 0] = both[0]
    for i in range(4):
        b1[xy, 1 + i] = jnp.where(core == 0, both[1 + i], both[5 + i])
    b2[z] = group_sum(b1, xy, plane_peers, 16, sum_send.at[4], sum_recv.at[4])
    total = group_sum(b2, z, z_peers, 16, sum_send.at[5], sum_recv.at[5])
    c2 = coefficients(total[0])
    for h in range(2):
        first_half = total[1 + h] + c2[0] * total[3 + h]
        second_half = c2[1] * total[1 + h] + c2[2] * total[3 + h]
        b3[core, h] = jnp.where(core == 0, first_half, second_half)

    def write_early():
        for r in range(ROWS):
            e = HALO + r
            v = c2[0] * u[3, e] + c2[1] * u[4, e] + c2[2] * u[5, e]
            out_early[:, r, :] = v[:, :COLS]
        stores[1].start()

    bank_rows = group_sum(b3, core, core_peer, 2, sum_send.at[6], sum_recv.at[6], write_early)
    out_bank[:, :128] = bank_rows[0]
    out_bank[:, 128:] = bank_rows[1]
    stores[2].start()
    for c in halo:
        c.wait_send()
    for c in pending:
        c.wait_send()
    for c in stores:
        c.wait()


def finish(late, early, bank, out_late, out_early, out_bank, late_v, early_v, bank_v, sem):
    ins = [
        pltpu.make_async_copy(src, dst, sem.at[n])
        for n, (src, dst) in enumerate(((late, late_v), (early, early_v), (bank, bank_v)))
    ]
    outs = [
        pltpu.make_async_copy(src, dst, sem.at[3 + n])
        for n, (src, dst) in enumerate(((late_v, out_late), (early_v, out_early), (bank_v, out_bank)))
    ]
    for c in ins:
        c.start()
    for c, d in zip(ins, outs):
        c.wait()
        d.start()
    for c in outs:
        c.wait()


def on_device(
    cond_x, cond_y, via_cond, capacity, class_map, via_mask, bank_map,
    source_late, source_early, rate_late, rate_early,
):
    f32, i32 = jnp.float32, jnp.int32
    hbm = pl.BlockSpec(memory_space=pltpu.HBM)
    dma = pltpu.SemaphoreType.DMA
    block = jax.ShapeDtypeStruct((LAYERS, ROWS, COLS), f32)
    shapes = (block, block, jax.ShapeDtypeStruct((1, BANKS), f32))
    wide = (SPAN, LAYERS, WIDE)
    field = pltpu.VMEM((LAYERS, ROWS, COLS), f32)
    results = pl.pallas_call(
        kernel,
        out_shape=shapes,
        in_specs=[hbm] * 11,
        out_specs=(hbm,) * 3,
        scratch_shapes=[
            field, field, pltpu.VMEM((1, BANKS), f32),
            field, field, field, field,
            pltpu.VMEM((ROWS, COLS), i32),
            pltpu.VMEM((LAYERS, NCLASS), i32),
            pltpu.VMEM((LAYERS, 16), i32),
            field, field, field, field,
            pltpu.VMEM((FIELDS,) + wide, f32),
            pltpu.VMEM((ROWS, LAYERS, 128), f32),
            pltpu.VMEM((ROWS, LAYERS, 128), f32),
            pltpu.VMEM((SPAN, LAYERS, 128), f32),
            pltpu.VMEM((SPAN, LAYERS, 128), f32),
            pltpu.VMEM((SPAN, LAYERS, 128), f32),
            pltpu.VMEM((SPAN, LAYERS, 128), f32),
            pltpu.VMEM((LAYERS, COLS), f32),
            pltpu.VMEM((LAYERS, 128), f32),
            pltpu.VMEM((LAYERS, 128), f32),
            pltpu.VMEM((6,) + wide, f32),
            pltpu.VMEM((2,) + wide, f32),
            pltpu.VMEM((6,) + wide, f32),
            pltpu.VMEM((6,) + wide, f32),
            pltpu.VMEM((3, 2 * HALO, LAYERS, WIDE), f32),
            pltpu.VMEM((3, 4) + wide, f32),
            pltpu.VMEM((2, 4) + wide, f32),
            pltpu.VMEM(wide, f32),
            pltpu.VMEM(wide, f32),
            pltpu.VMEM((2, 1, 1, 128), f32),
            pltpu.VMEM((16, 1, 1, 128), f32),
            pltpu.VMEM((16, 1, 1, 128), f32),
            pltpu.VMEM((2, 9, 1, 128), f32),
            pltpu.VMEM((16, 5, 1, 128), f32),
            pltpu.VMEM((16, 5, 1, 128), f32),
            pltpu.VMEM((2, 2, 1, 128), f32),
            dma((11,)),
            dma((3,)),
            dma((19,)),
            dma((19,)),
            dma((10, 2)),
            dma((10, 2)),
            dma((3, 2)),
            dma((3, 2)),
            dma((7,)),
            dma((7,)),
            pltpu.SemaphoreType.REGULAR((2,)),
        ],
        compiler_params=pltpu.CompilerParams(
            collective_id=0, has_side_effects=True, vmem_limit_bytes=60 << 20
        ),
        name="adjoint_steps",
    )(
        cond_x, cond_y, via_cond, capacity, class_map, via_mask, bank_map.reshape(LAYERS, 16),
        source_late, source_early, rate_late, rate_early,
    )
    late, early, bank = pl.pallas_call(
        finish,
        out_shape=shapes,
        in_specs=[hbm] * 3,
        out_specs=(hbm,) * 3,
        scratch_shapes=[field, field, pltpu.VMEM((1, BANKS), f32), dma((6,))],
        compiler_params=pltpu.CompilerParams(vmem_limit_bytes=60 << 20),
        name="write_results",
    )(*results)
    return late, early, bank.reshape(BANKS)


def solution(mesh):
    block = P(None, "tile", "layer")
    in_specs = (block,) * 4 + (P("tile", "layer"), P()) + (block,) * 5
    return jax.shard_map(
        on_device, mesh=mesh, in_specs=in_specs, out_specs=(block, block, P()), check_vma=False
    )
```

```python
import functools

import jax
import jax.numpy as jnp
from jax import lax
from jax.experimental import pallas as pl
from jax.experimental.pallas import tpu as pltpu
from jax.sharding import PartitionSpec as P

MESH = pl.DeviceIdType.MESH
NCLASS = 8
DCOLS = 16
BANKS = 256
LAYERS = 8
ROWS = 4
COLS = 256
HALO = 4
SPAN = ROWS + 2 * HALO
WIDE = COLS + 128
EDGE = 24
FIELDS = 6
EAST, SOUTH, UP, CAP, LATE, EARLY = range(FIELDS)

lower_edge = 0.05
upper_edge = 2.0
centre = (lower_edge + upper_edge) / 2.0
half = (upper_edge - lower_edge) / 2.0
sigma = centre / half


def sweep_constants():
    out = []
    rho = 1.0 / sigma
    for _ in range(3):
        nxt = 1.0 / (2.0 * sigma - rho)
        out.append((nxt * rho, 2.0 * nxt / half))
        rho = nxt
    return out


def next_col(v):
    return pltpu.roll(v, WIDE - 1, 1)


def prev_col(v):
    return pltpu.roll(v, 1, 1)


def next_layer(v):
    return pltpu.roll(v, LAYERS - 1, 0)


def prev_layer(v):
    return pltpu.roll(v, 1, 0)


def neighbours(z, coef, r):
    v = z[r]
    acc = coef[0, r] * next_col(v) + coef[1, r] * prev_col(v)
    acc = acc + (coef[2, r] * z[r + 1] + coef[3, r] * z[r - 1])
    return acc + (coef[4, r] * next_layer(v) + coef[5, r] * prev_layer(v))


def krylov_coefficients(mu):
    zero = jnp.zeros_like(mu[0])
    one = zero + 1.0
    nu = [mu[s] - mu[s + 1] for s in range(5)]

    def form(c, moments):
        total = None
        for s in range(2 * len(c) - 1):
            w = None
            for i in range(len(c)):
                j = s - i
                if 0 <= j < len(c):
                    w = c[i] * c[j] if w is None else w + c[i] * c[j]
            total = w * moments[s] if total is None else total + w * moments[s]
        return total

    def plus(a, b, scale):
        n = max(len(a), len(b))
        a, b = a + [zero] * (n - len(a)), b + [zero] * (n - len(b))
        return [p + scale * q for p, q in zip(a, b)]

    res, sea, sol = [one], [one], []
    gamma = mu[0]
    for step in range(3):
        alpha = gamma / form(sea, nu)
        sol = plus(sol, sea, alpha)
        if step < 2:
            res = plus(plus(res, sea, -alpha), [zero] + sea, alpha)
            new = form(res, mu)
            sea = plus(res, sea, new / gamma)
            gamma = new
    return sol


def kernel(
    cond_x_in, cond_y_in, via_in, cap_in, cls_in, mask_in, bank_in, late_in, early_in, rate_late_in, rate_early_in,
    late_out, early_out, bank_out,
    out_late, out_early, out_bank, cond_x, cond_y, via, cap, cls, mask, bank, late, early, rate_late, rate_early,
    ext, pack_r, pack_l, col_r, col_l, early_r, early_l, sx, sx_r, sx_l, coef, diag, g, u, uh, pg, pu, z1, z2,
    a0, a1, a2, b0, b1, b2,
    load_sem, store_sem, halo_send, halo_recv, mid_send, mid_recv, ush_send, ush_recv, sum_send, sum_recv, reach,
):
    loads = [
        pltpu.make_async_copy(src, dst, load_sem.at[n])
        for n, (src, dst) in enumerate((
            (cond_x_in, cond_x), (cond_y_in, cond_y), (via_in, via), (cap_in, cap), (cls_in, cls),
            (mask_in, mask), (late_in, late), (early_in, early), (bank_in, bank),
            (rate_late_in, rate_late), (rate_early_in, rate_early),
        ))
    ]
    for c in loads:
        c.start()

    lay = lax.axis_index("layer")
    til = lax.axis_index("tile")
    lays = lax.axis_size("layer")
    tils = lax.axis_size("tile")
    y, core = lay // 2, lay % 2
    z, x = til // 4, til % 4

    around = {
        (dl, dt): ((lay + dl + lays) % lays, (til + dt + tils) % tils)
        for dt in (-16, -8, -4, -2, -1, 0, 1, 2, 4, 8, 16)
        for dl in ((-1, 0, 1) if -2 <= dt <= 2 else (0,))
    }

    def at(dl, dt):
        return around[dl, dt]

    core_peer = [(lay + 1 - 2 * core, til)]
    plane_peers = [
        (((y + dy) % 4) * 2 + core, z * 4 + (x + dx) % 4)
        for dy in (2, 1, 3, 0) for dx in (2, 1, 3, 0) if (dy, dx) != (0, 0)
    ]
    z_peers = [
        (lay, ((z + i) % 16) * 4 + x) for i in sorted(range(1, 16), key=lambda i: -min(i, 16 - i))
    ]

    barrier = pltpu.get_barrier_semaphore()
    greet = [at(dl, dt) for dt in (-2, -1, 0, 1, 2) for dl in (-1, 0, 1) if (dl, dt) != (0, 0)]
    greet += plane_peers + [at(0, 4 * dz) for dz in (-2, 2, -1, 1)]
    for d in greet:
        pl.semaphore_signal(barrier, inc=1, device_id=d, device_id_type=MESH)

    lane = lax.broadcasted_iota(jnp.int32, (LAYERS, COLS), 1)
    layer = lax.broadcasted_iota(jnp.int32, (LAYERS, COLS), 0)
    last_col = jnp.logical_and(lane == COLS - 1, lay == lays - 1)
    top = layer == LAYERS - 1
    for c in loads[:8]:
        c.wait()
    masks = mask[...].astype(jnp.float32)
    for r in range(ROWS):
        e = HALO + r
        ext[EAST, e, :, :COLS] = jnp.where(last_col, 0.0, cond_x[:, r, :])
        south = cond_y[:, r, :]
        if r == ROWS - 1:
            south = jnp.where(til == tils - 1, 0.0, south)
        ext[SOUTH, e, :, :COLS] = south
        kind = jnp.broadcast_to(cls[r : r + 1, :], (LAYERS, COLS))
        opened = jnp.zeros((LAYERS, COLS), jnp.float32)
        for k in range(NCLASS):
            opened = jnp.where(kind == k, masks[:, k : k + 1], opened)
        ext[UP, e, :, :COLS] = jnp.where(top, 0.0, via[:, r, :] * opened)
        ext[CAP, e, :, :COLS] = cap[:, r, :]
        ext[LATE, e, :, :COLS] = late[:, r, :]
        ext[EARLY, e, :, :COLS] = early[:, r, :]
        lane128 = lax.broadcasted_iota(jnp.int32, (LAYERS, 128), 1)
        right = jnp.zeros((LAYERS, 128), jnp.float32)
        left = right
        for f in range(EARLY):
            here = jnp.logical_and(lane128 >= EDGE * f, lane128 < EDGE * (f + 1))
            v = ext[f, e, :, :128]
            right = jnp.where(here, pltpu.roll(v, EDGE * f, 1) if f else v, right)
            v = ext[f, e, :, COLS - 128 : COLS]
            left = jnp.where(here, pltpu.roll(v, (EDGE * (f + 1)) % 128, 1), left)
        pack_r[r] = right
        pack_l[r] = left

    pl.semaphore_wait(barrier, len(greet))
    for dz in (-2, 2):
        pl.semaphore_signal(reach.at[0], inc=1, device_id=at(0, 4 * dz), device_id_type=MESH)

    own = pl.ds(HALO, ROWS)
    halo = []

    def send(src, dst, peer):
        n = len(halo)
        halo.append(
            pltpu.make_async_remote_copy(
                src_ref=src, dst_ref=dst, send_sem=halo_send.at[n], recv_sem=halo_recv.at[n],
                device_id=peer, device_id_type=MESH,
            )
        )
        halo[-1].start()

    def send_rows(first, count, dt, row):
        fields = pl.ds(first, count)
        send(
            ext.at[fields, own, :, pl.ds(0, COLS)],
            ext.at[fields, pl.ds(row, ROWS), :, pl.ds(0, COLS)],
            at(0, dt),
        )

    def send_columns(dt, row):
        send(pack_r, col_r.at[pl.ds(row, ROWS)], at(-1, dt))
        send(pack_l, col_l.at[pl.ds(row, ROWS)], at(1, dt))

    near = ((1, 0), (-1, HALO + ROWS))
    last = ext.at[SOUTH, HALO + ROWS - 1]
    send(last.at[:, pl.ds(0, 128)], sx_r, at(-1, 2))
    send(last.at[:, pl.ds(COLS - 128, 128)], sx_l, at(1, 2))
    send(last.at[:, pl.ds(0, COLS)], sx, at(0, 2))
    for dt, row in near:
        send_columns(dt, row)
    for dt, row in near:
        send_rows(0, EARLY, dt, row)
    send_columns(0, HALO)
    first = len(halo)
    for c in halo:
        c.wait_recv()
    for dt, row in near + ((0, HALO),):
        if dt:
            send_rows(EARLY, 1, dt, row)
        send(ext.at[EARLY, own, :, pl.ds(0, 128)], early_r.at[pl.ds(row, ROWS)], at(-1, dt))
        send(
            ext.at[EARLY, own, :, pl.ds(COLS - 128, 128)], early_l.at[pl.ds(row, ROWS)], at(1, dt)
        )
    pl.semaphore_wait(reach.at[0], 2)
    for dz in (-4, 4):
        pl.semaphore_signal(reach.at[1], inc=1, device_id=at(0, 4 * dz), device_id_type=MESH)

    slot = lax.broadcasted_iota(jnp.int32, (LAYERS, 128), 1)

    for r in range(SPAN):
        to_right, to_left = col_r[r], col_l[r]
        for f in range(EARLY):
            a = pltpu.roll(to_right, (128 - EDGE * f) % 128, 1)
            b = pltpu.roll(to_left, (256 - EDGE * (f + 1)) % 128, 1)
            rest = jnp.where(slot >= 128 - EDGE, b, 1.0 if f == CAP else 0.0)
            ext[f, r, :, COLS:] = jnp.where(slot < EDGE, a, rest)
    north = jnp.concatenate([sx[...], jnp.where(slot < 64, sx_r[...], sx_l[...])], axis=1)
    for r in range(SPAN):
        east = ext[EAST, r]
        west = prev_col(east)
        south = ext[SOUTH, r]
        upward = ext[UP, r]
        downward = prev_layer(upward)
        d = ext[CAP, r] + east + west + south + north + upward + downward
        inv = 1.0 / d
        diag[0, r] = d
        diag[1, r] = inv
        g[0, r] = ext[LATE, r] * inv
        for i, c in enumerate((east, west, south, north, upward, downward)):
            coef[i, r] = c * inv
        north = south

    (q1, p1), (q2, p2), (q3, p3) = sweep_constants()

    def iterate(gi, ui, gn):
        for r in range(1, SPAN - 1):
            z1[r] = ((1.0 + q1 - p1) / centre + p1) * gi[r] + (p1 / centre) * neighbours(gi, coef, r)
        for r in range(2, SPAN - 2):
            z2[r] = (1.0 + q2 - p2) * z1[r] + (p2 - q2 / centre) * gi[r] + p2 * neighbours(z1, coef, r)
        for r in range(3, SPAN - 3):
            ui[r] = (
                (1.0 + q3 - p3) * z2[r] - q3 * z1[r] + p3 * gi[r] + p3 * neighbours(z2, coef, r)
            )
        for r in own_rows:
            gn[r] = gi[r] - ui[r] + neighbours(ui, coef, r)

    own_rows = range(HALO, HALO + ROWS)
    pending = []

    def send_block(src, above, below, ssem, rsem):
        copies = []
        for n, (dt, dst) in enumerate(((1, above), (-1, below))):
            c = pltpu.make_async_remote_copy(
                src_ref=src.at[own], dst_ref=dst, send_sem=ssem.at[n], recv_sem=rsem.at[n],
                device_id=at(0, dt), device_id_type=MESH,
            )
            c.start()
            copies.append(c)
        pending.extend(copies)
        return copies

    def send_g(ref, n):
        return send_block(
            ref, ref.at[pl.ds(0, HALO)], ref.at[pl.ds(HALO + ROWS, HALO)], mid_send.at[n], mid_recv.at[n]
        )

    def send_u(i):
        return send_block(
            u.at[i], uh.at[i, pl.ds(0, HALO)], uh.at[i, pl.ds(HALO, HALO)],
            ush_send.at[i], ush_recv.at[i],
        )

    def arrive(copies):
        for c in copies:
            c.wait_recv()

    def add_products(parts, i, gi, ui, gn):
        for r in own_rows:
            du = (diag[0, r] * ui[r])[:, :COLS]
            for k, ref in ((2 * i, gi), (2 * i + 1, gn)):
                term = du * ref[r][:, :COLS]
                parts[k] = term if parts[k] is None else parts[k] + term

    def moment_row(parts):
        lanes = lax.broadcasted_iota(jnp.int32, (1, 128), 1)
        row = jnp.zeros((1, 128), jnp.float32)
        for k, p in enumerate(parts):
            row = jnp.where(lanes == k, jnp.sum(p, axis=(0, 1), keepdims=True), row)
        return row

    def group_sum(buf, me, peers, n, ssem, rsem, beside=None):
        for d in peers:
            pltpu.make_async_remote_copy(
                src_ref=buf.at[me], dst_ref=buf.at[me], send_sem=ssem, recv_sem=rsem,
                device_id=d, device_id_type=MESH,
            ).start()
        most = buf.at[pl.ds(0, n - 1)]
        whole = pltpu.make_async_remote_copy(
            src_ref=most, dst_ref=most, send_sem=ssem, recv_sem=rsem,
            device_id=peers[0], device_id_type=MESH,
        )
        if beside is not None:
            beside()
        whole.wait_recv()
        pending.append(whole)
        total = buf[0]
        for i in range(1, n):
            total = total + buf[i]
        return total

    def all_sum(bufs, base, beside=(None, None, None)):
        c, p, w = bufs
        xy = y * 4 + x
        send, recv = sum_send.at, sum_recv.at
        p[xy] = group_sum(c, core, core_peer, 2, send[base], recv[base], beside[0])
        w[z] = group_sum(p, xy, plane_peers, 16, send[base + 1], recv[base + 1], beside[1])
        return group_sum(w, z, z_peers, 16, send[base + 2], recv[base + 2], beside[2])

    def coefficients(row):
        lanes = lax.broadcasted_iota(jnp.int32, (1, 128), 1)
        mu = [
            jnp.sum(jnp.where(lanes == k, row, 0.0), axis=(0, 1), keepdims=True) for k in range(6)
        ]
        return krylov_coefficients(mu)

    parts = [None] * 6
    iterate(g.at[0], u.at[0], g.at[1])
    moving = send_g(g.at[1], 0)
    shared = [send_u(0)]
    add_products(parts, 0, g.at[0], u.at[0], g.at[1])
    arrive(moving)
    iterate(g.at[1], u.at[1], g.at[2])
    moving = send_g(g.at[2], 1)
    shared.append(send_u(1))
    add_products(parts, 1, g.at[1], u.at[1], g.at[2])
    traded = {}

    def part_step(step, n):
        if step:
            arrive(traded[0, n])
        iterate(pg.at[step, n], pu.at[step, n], pg.at[step + 1, n])
        traded[step, n] = send_g(pg.at[step + 1, n], 2 + 4 * step + n)

    def source_part():
        arrive(halo[first:])
        for r in range(SPAN):
            ext[EARLY, r, :, COLS:] = jnp.where(slot < 64, early_r[r], early_l[r])
            pg[0, 0, r] = ext[EARLY, r] * diag[1, r]
        part_step(0, 0)

    def field_part(i):
        arrive(shared[i])
        for r in range(SPAN):
            if r in own_rows:
                v = u[i, r]
            else:
                v = uh[i, r if r < HALO else r - ROWS]
            pg[0, 1 + i, r] = ext[CAP, r] * diag[1, r] * v
        part_step(0, 1 + i)

    source_part()
    field_part(0)
    arrive(moving)
    iterate(g.at[2], u.at[2], z1)
    shared.append(send_u(2))
    add_products(parts, 2, g.at[2], u.at[2], z1)
    a0[core] = moment_row(parts).reshape(1, 1, 128)
    for c in loads[8:10]:
        c.wait()
    pl.semaphore_wait(reach.at[1], 2)

    def beside_plane():
        field_part(1)
        field_part(2)

    def beside_z():
        for n in (0, 1, 2, 3):
            part_step(1, n)

    row = all_sum((a0, a1, a2), 0, (None, beside_plane, beside_z))
    c1 = coefficients(row.reshape(1, 128))

    def added(ref, r):
        return ref[0, r] + c1[0] * ref[1, r] + c1[1] * ref[2, r] + c1[2] * ref[3, r]

    for n in range(4):
        arrive(traded[1, n])
    for r in range(SPAN):
        g[5, r] = added(pg.at[2], r)
    iterate(g.at[5], u.at[5], z1)
    held = jnp.zeros((LAYERS, COLS), jnp.float32)
    for r in own_rows:
        g[3, r] = added(pg.at[0], r)
        g[4, r] = added(pg.at[1], r)
        u[3, r] = added(pu.at[0], r)
        u[4, r] = added(pu.at[1], r)
        v = c1[0] * u[0, r] + c1[1] * u[1, r] + c1[2] * u[2, r]
        out_late[:, r - HALO, :] = v[:, :COLS]
        held = held + v[:, :COLS] * rate_late[:, r - HALO, :]
    stores = [
        pltpu.make_async_copy(src, dst, store_sem.at[n])
        for n, (src, dst) in enumerate(
            ((out_late, late_out), (out_early, early_out), (out_bank, bank_out))
        )
    ]
    stores[0].start()

    parts = [None] * 6
    add_products(parts, 0, g.at[3], u.at[3], g.at[4])
    add_products(parts, 1, g.at[4], u.at[4], g.at[5])
    add_products(parts, 2, g.at[5], u.at[5], z1)
    for c in loads[10:]:
        c.wait()
    moments = moment_row(parts)
    terms = [held]
    for i in (3, 4, 5):
        t = None
        for r in own_rows:
            w = u[i, r][:, :COLS] * rate_early[:, r - HALO, :]
            t = w if t is None else t + w
        terms.append(t)

    hi = lax.Precision.HIGHEST
    f32 = jnp.float32

    def iota(shape, dim):
        return lax.broadcasted_iota(jnp.int32, shape, dim)

    spread = (iota((16, 128), 0) == iota((16, 128), 1) % 16).astype(f32)
    bank_of = jnp.dot(bank[...].astype(f32), spread, precision=hi, preferred_element_type=f32)
    mine = iota((LAYERS, 128), 0) == iota((LAYERS, 128), 1) // 16
    bank_row = jnp.sum(jnp.where(mine, bank_of, 0.0), axis=0, keepdims=True)
    chosen = (iota((BANKS, 128), 0) == (bank_row + 0.5).astype(jnp.int32)).astype(f32)
    tile_of = (iota((COLS, 128), 0) // DCOLS == iota((COLS, 128), 1) % 16).astype(f32)
    tiles = jnp.dot(jnp.concatenate(terms, axis=0), tile_of, precision=hi, preferred_element_type=f32)
    tiles = jnp.where(iota((4 * LAYERS, 128), 0) % LAYERS == iota((4 * LAYERS, 128), 1) // 16, tiles, 0.0)
    sums = lax.dot_general(
        tiles, chosen, (((1,), (1,)), ((), ())), precision=hi, preferred_element_type=f32
    )
    for i in range(4):
        s = jnp.sum(sums[i * LAYERS : (i + 1) * LAYERS], axis=0, keepdims=True)
        b0[core, 2 * i] = s[:, :128]
        b0[core, 2 * i + 1] = s[:, 128:]
    b0[core, 8] = moments

    total = all_sum((b0, b1, b2), 3)
    c2 = coefficients(total[8])
    for h in range(2):
        out_bank[:, h * 128 : (h + 1) * 128] = (
            total[h] + c2[0] * total[2 + h] + c2[1] * total[4 + h] + c2[2] * total[6 + h]
        )
    for r in range(ROWS):
        e = HALO + r
        v = c2[0] * u[3, e] + c2[1] * u[4, e] + c2[2] * u[5, e]
        out_early[:, r, :] = v[:, :COLS]
    stores[1].start()
    stores[2].start()
    for c in halo:
        c.wait_send()
    for c in pending:
        c.wait_send()
    for c in stores:
        c.wait()


def finish(late, early, bank, out_late, out_early, out_bank, late_v, early_v, bank_v, sem):
    ins = [
        pltpu.make_async_copy(src, dst, sem.at[n])
        for n, (src, dst) in enumerate(((late, late_v), (early, early_v), (bank, bank_v)))
    ]
    outs = [
        pltpu.make_async_copy(src, dst, sem.at[3 + n])
        for n, (src, dst) in enumerate(((late_v, out_late), (early_v, out_early), (bank_v, out_bank)))
    ]
    for c in ins:
        c.start()
    for c, d in zip(ins, outs):
        c.wait()
        d.start()
    for c in outs:
        c.wait()


def on_device(
    cond_x, cond_y, via_cond, capacity, class_map, via_mask, bank_map,
    source_late, source_early, rate_late, rate_early,
):
    f32, i32 = jnp.float32, jnp.int32
    hbm = pl.BlockSpec(memory_space=pltpu.HBM)
    dma = pltpu.SemaphoreType.DMA
    block = jax.ShapeDtypeStruct((LAYERS, ROWS, COLS), f32)
    shapes = (block, block, jax.ShapeDtypeStruct((1, BANKS), f32))
    wide = (SPAN, LAYERS, WIDE)
    field = pltpu.VMEM((LAYERS, ROWS, COLS), f32)
    results = pl.pallas_call(
        kernel,
        out_shape=shapes,
        in_specs=[hbm] * 11,
        out_specs=(hbm,) * 3,
        scratch_shapes=[
            field, field, pltpu.VMEM((1, BANKS), f32),
            field, field, field, field,
            pltpu.VMEM((ROWS, COLS), i32),
            pltpu.VMEM((LAYERS, NCLASS), i32),
            pltpu.VMEM((LAYERS, 16), i32),
            field, field, field, field,
            pltpu.VMEM((FIELDS,) + wide, f32),
            pltpu.VMEM((ROWS, LAYERS, 128), f32),
            pltpu.VMEM((ROWS, LAYERS, 128), f32),
            pltpu.VMEM((SPAN, LAYERS, 128), f32),
            pltpu.VMEM((SPAN, LAYERS, 128), f32),
            pltpu.VMEM((SPAN, LAYERS, 128), f32),
            pltpu.VMEM((SPAN, LAYERS, 128), f32),
            pltpu.VMEM((LAYERS, COLS), f32),
            pltpu.VMEM((LAYERS, 128), f32),
            pltpu.VMEM((LAYERS, 128), f32),
            pltpu.VMEM((6,) + wide, f32),
            pltpu.VMEM((2,) + wide, f32),
            pltpu.VMEM((6,) + wide, f32),
            pltpu.VMEM((6,) + wide, f32),
            pltpu.VMEM((3, 2 * HALO, LAYERS, WIDE), f32),
            pltpu.VMEM((3, 4) + wide, f32),
            pltpu.VMEM((2, 4) + wide, f32),
            pltpu.VMEM(wide, f32),
            pltpu.VMEM(wide, f32),
            pltpu.VMEM((2, 1, 1, 128), f32),
            pltpu.VMEM((16, 1, 1, 128), f32),
            pltpu.VMEM((16, 1, 1, 128), f32),
            pltpu.VMEM((2, 9, 1, 128), f32),
            pltpu.VMEM((16, 9, 1, 128), f32),
            pltpu.VMEM((16, 9, 1, 128), f32),
            dma((11,)),
            dma((3,)),
            dma((19,)),
            dma((19,)),
            dma((10, 2)),
            dma((10, 2)),
            dma((3, 2)),
            dma((3, 2)),
            dma((7,)),
            dma((7,)),
            pltpu.SemaphoreType.REGULAR((2,)),
        ],
        compiler_params=pltpu.CompilerParams(
            collective_id=0, has_side_effects=True, vmem_limit_bytes=60 << 20
        ),
        name="adjoint_steps",
    )(
        cond_x, cond_y, via_cond, capacity, class_map, via_mask, bank_map.reshape(LAYERS, 16),
        source_late, source_early, rate_late, rate_early,
    )
    late, early, bank = pl.pallas_call(
        finish,
        out_shape=shapes,
        in_specs=[hbm] * 3,
        out_specs=(hbm,) * 3,
        scratch_shapes=[field, field, pltpu.VMEM((1, BANKS), f32), dma((6,))],
        compiler_params=pltpu.CompilerParams(vmem_limit_bytes=60 << 20),
        name="write_results",
    )(*results)
    return late, early, bank.reshape(BANKS)


def solution(mesh):
    block = P(None, "tile", "layer")
    in_specs = (block,) * 4 + (P("tile", "layer"), P()) + (block,) * 5
    return jax.shard_map(
        on_device, mesh=mesh, in_specs=in_specs, out_specs=(block, block, P()), check_vma=False
    )
```

```python
import functools

import jax
import jax.numpy as jnp
from jax import lax
from jax.experimental import pallas as pl
from jax.experimental.pallas import tpu as pltpu
from jax.sharding import PartitionSpec as P

MESH = pl.DeviceIdType.MESH
NCLASS = 8
DCOLS = 16
BANKS = 256
LAYERS = 8
ROWS = 4
COLS = 256
HALO = 4
SPAN = ROWS + 2 * HALO
WIDE = COLS + 128
EDGE = 24
FIELDS = 6
EAST, SOUTH, UP, CAP, LATE, EARLY = range(FIELDS)

lower_edge = 0.05
upper_edge = 2.0
centre = (lower_edge + upper_edge) / 2.0
half = (upper_edge - lower_edge) / 2.0
sigma = centre / half


def sweep_constants():
    out = []
    rho = 1.0 / sigma
    for _ in range(3):
        nxt = 1.0 / (2.0 * sigma - rho)
        out.append((nxt * rho, 2.0 * nxt / half))
        rho = nxt
    return out


def next_col(v):
    return pltpu.roll(v, WIDE - 1, 1)


def prev_col(v):
    return pltpu.roll(v, 1, 1)


def next_layer(v):
    return pltpu.roll(v, LAYERS - 1, 0)


def prev_layer(v):
    return pltpu.roll(v, 1, 0)


def neighbours(z, coef, r):
    v = z[r]
    acc = coef[0, r] * next_col(v) + coef[1, r] * prev_col(v)
    acc = acc + (coef[2, r] * z[r + 1] + coef[3, r] * z[r - 1])
    return acc + (coef[4, r] * next_layer(v) + coef[5, r] * prev_layer(v))


def krylov_coefficients(mu):
    zero = jnp.zeros_like(mu[0])
    one = zero + 1.0
    nu = [mu[s] - mu[s + 1] for s in range(5)]

    def form(c, moments):
        total = None
        for s in range(2 * len(c) - 1):
            w = None
            for i in range(len(c)):
                j = s - i
                if 0 <= j < len(c):
                    w = c[i] * c[j] if w is None else w + c[i] * c[j]
            total = w * moments[s] if total is None else total + w * moments[s]
        return total

    def plus(a, b, scale):
        n = max(len(a), len(b))
        a, b = a + [zero] * (n - len(a)), b + [zero] * (n - len(b))
        return [p + scale * q for p, q in zip(a, b)]

    res, sea, sol = [one], [one], []
    gamma = mu[0]
    for step in range(3):
        alpha = gamma / form(sea, nu)
        sol = plus(sol, sea, alpha)
        if step < 2:
            res = plus(plus(res, sea, -alpha), [zero] + sea, alpha)
            new = form(res, mu)
            sea = plus(res, sea, new / gamma)
            gamma = new
    return sol


def kernel(
    cond_x_in, cond_y_in, via_in, cap_in, cls_in, mask_in, bank_in, late_in, early_in, rate_late_in, rate_early_in,
    late_out, early_out, bank_out,
    out_late, out_early, out_bank, cond_x, cond_y, via, cap, cls, mask, bank, late, early, rate_late, rate_early,
    ext, pack_r, pack_l, col_r, col_l, early_r, early_l, sx, sx_r, sx_l, coef, diag, g, u, uh, pg, pu, z1, z2,
    a0, a1, a2, b0, b1, b2,
    load_sem, store_sem, halo_send, halo_recv, mid_send, mid_recv, ush_send, ush_recv, sum_send, sum_recv, reach,
):
    loads = [
        pltpu.make_async_copy(src, dst, load_sem.at[n])
        for n, (src, dst) in enumerate((
            (cond_x_in, cond_x), (cond_y_in, cond_y), (via_in, via), (cap_in, cap), (cls_in, cls),
            (mask_in, mask), (late_in, late), (early_in, early), (bank_in, bank),
            (rate_late_in, rate_late), (rate_early_in, rate_early),
        ))
    ]
    lay = lax.axis_index("layer")
    til = lax.axis_index("tile")
    lays = lax.axis_size("layer")
    tils = lax.axis_size("tile")
    y, core = lay // 2, lay % 2
    z, x = til // 4, til % 4

    around = {
        (dl, dt): ((lay + dl + lays) % lays, (til + dt + tils) % tils)
        for dt in (-16, -8, -4, -2, -1, 0, 1, 2, 4, 8, 16)
        for dl in ((-1, 0, 1) if -2 <= dt <= 2 else (0,))
    }

    def at(dl, dt):
        return around[dl, dt]

    core_peer = [(lay + 1 - 2 * core, til)]
    plane_peers = [
        (((y + dy) % 4) * 2 + core, z * 4 + (x + dx) % 4)
        for dy in (2, 1, 3, 0) for dx in (2, 1, 3, 0) if (dy, dx) != (0, 0)
    ]
    z_peers = [
        (lay, ((z + i) % 16) * 4 + x) for i in sorted(range(1, 16), key=lambda i: -min(i, 16 - i))
    ]

    barrier = pltpu.get_barrier_semaphore()
    near_peers = [at(dl, dt) for dt in (1, -1, 0, 2, -2) for dl in (0, 1, -1) if (dl, dt) != (0, 0)]
    near_peers += [at(0, 4 * dz) for dz in (-2, 2, -1, 1)]
    greet = near_peers + plane_peers

    def hello(peers):
        for d in peers:
            pl.semaphore_signal(barrier, inc=1, device_id=d, device_id_type=MESH)

    hello(near_peers)
    for c in loads:
        c.start()
    hello(plane_peers)

    lane = lax.broadcasted_iota(jnp.int32, (LAYERS, COLS), 1)
    layer = lax.broadcasted_iota(jnp.int32, (LAYERS, COLS), 0)
    last_col = jnp.logical_and(lane == COLS - 1, lay == lays - 1)
    top = layer == LAYERS - 1
    for c in loads[:8]:
        c.wait()
    masks = mask[...].astype(jnp.float32)
    for r in range(ROWS):
        e = HALO + r
        ext[EAST, e, :, :COLS] = jnp.where(last_col, 0.0, cond_x[:, r, :])
        south = cond_y[:, r, :]
        if r == ROWS - 1:
            south = jnp.where(til == tils - 1, 0.0, south)
        ext[SOUTH, e, :, :COLS] = south
        kind = jnp.broadcast_to(cls[r : r + 1, :], (LAYERS, COLS))
        opened = jnp.zeros((LAYERS, COLS), jnp.float32)
        for k in range(NCLASS):
            opened = jnp.where(kind == k, masks[:, k : k + 1], opened)
        ext[UP, e, :, :COLS] = jnp.where(top, 0.0, via[:, r, :] * opened)
        ext[CAP, e, :, :COLS] = cap[:, r, :]
        ext[LATE, e, :, :COLS] = late[:, r, :]
        ext[EARLY, e, :, :COLS] = early[:, r, :]
        lane128 = lax.broadcasted_iota(jnp.int32, (LAYERS, 128), 1)
        right = jnp.zeros((LAYERS, 128), jnp.float32)
        left = right
        for f in range(EARLY):
            here = jnp.logical_and(lane128 >= EDGE * f, lane128 < EDGE * (f + 1))
            v = ext[f, e, :, :128]
            right = jnp.where(here, pltpu.roll(v, EDGE * f, 1) if f else v, right)
            v = ext[f, e, :, COLS - 128 : COLS]
            left = jnp.where(here, pltpu.roll(v, (EDGE * (f + 1)) % 128, 1), left)
        pack_r[r] = right
        pack_l[r] = left

    pl.semaphore_wait(barrier, len(greet))
    for dz in (-2, 2):
        pl.semaphore_signal(reach.at[0], inc=1, device_id=at(0, 4 * dz), device_id_type=MESH)

    own = pl.ds(HALO, ROWS)
    halo = []

    def send(src, dst, peer):
        n = len(halo)
        halo.append(
            pltpu.make_async_remote_copy(
                src_ref=src, dst_ref=dst, send_sem=halo_send.at[n], recv_sem=halo_recv.at[n],
                device_id=peer, device_id_type=MESH,
            )
        )
        halo[-1].start()

    def send_rows(first, count, dt, row):
        fields = pl.ds(first, count)
        send(
            ext.at[fields, own, :, pl.ds(0, COLS)],
            ext.at[fields, pl.ds(row, ROWS), :, pl.ds(0, COLS)],
            at(0, dt),
        )

    def send_columns(dt, row):
        send(pack_r, col_r.at[pl.ds(row, ROWS)], at(-1, dt))
        send(pack_l, col_l.at[pl.ds(row, ROWS)], at(1, dt))

    near = ((1, 0), (-1, HALO + ROWS))
    last = ext.at[SOUTH, HALO + ROWS - 1]
    send(last.at[:, pl.ds(0, 128)], sx_r, at(-1, 2))
    send(last.at[:, pl.ds(COLS - 128, 128)], sx_l, at(1, 2))
    send(last.at[:, pl.ds(0, COLS)], sx, at(0, 2))
    for dt, row in near:
        send_columns(dt, row)
    for dt, row in near:
        send_rows(0, EARLY, dt, row)
    send_columns(0, HALO)
    first = len(halo)
    for c in halo:
        c.wait_recv()
    for dt, row in near + ((0, HALO),):
        if dt:
            send_rows(EARLY, 1, dt, row)
        send(ext.at[EARLY, own, :, pl.ds(0, 128)], early_r.at[pl.ds(row, ROWS)], at(-1, dt))
        send(
            ext.at[EARLY, own, :, pl.ds(COLS - 128, 128)], early_l.at[pl.ds(row, ROWS)], at(1, dt)
        )
    pl.semaphore_wait(reach.at[0], 2)
    for dz in (-4, 4):
        pl.semaphore_signal(reach.at[1], inc=1, device_id=at(0, 4 * dz), device_id_type=MESH)

    slot = lax.broadcasted_iota(jnp.int32, (LAYERS, 128), 1)

    for r in range(SPAN):
        to_right, to_left = col_r[r], col_l[r]
        for f in range(EARLY):
            a = pltpu.roll(to_right, (128 - EDGE * f) % 128, 1)
            b = pltpu.roll(to_left, (256 - EDGE * (f + 1)) % 128, 1)
            rest = jnp.where(slot >= 128 - EDGE, b, 1.0 if f == CAP else 0.0)
            ext[f, r, :, COLS:] = jnp.where(slot < EDGE, a, rest)
    north = jnp.concatenate([sx[...], jnp.where(slot < 64, sx_r[...], sx_l[...])], axis=1)
    for r in range(SPAN):
        east = ext[EAST, r]
        west = prev_col(east)
        south = ext[SOUTH, r]
        upward = ext[UP, r]
        downward = prev_layer(upward)
        d = ext[CAP, r] + east + west + south + north + upward + downward
        inv = 1.0 / d
        diag[0, r] = d
        diag[1, r] = inv
        g[0, r] = ext[LATE, r] * inv
        for i, c in enumerate((east, west, south, north, upward, downward)):
            coef[i, r] = c * inv
        north = south

    (q1, p1), (q2, p2), (q3, p3) = sweep_constants()

    def iterate(gi, ui, gn):
        for r in range(1, SPAN - 1):
            z1[r] = ((1.0 + q1 - p1) / centre + p1) * gi[r] + (p1 / centre) * neighbours(gi, coef, r)
        for r in range(2, SPAN - 2):
            z2[r] = (1.0 + q2 - p2) * z1[r] + (p2 - q2 / centre) * gi[r] + p2 * neighbours(z1, coef, r)
        for r in range(3, SPAN - 3):
            ui[r] = (
                (1.0 + q3 - p3) * z2[r] - q3 * z1[r] + p3 * gi[r] + p3 * neighbours(z2, coef, r)
            )
        for r in own_rows:
            gn[r] = gi[r] - ui[r] + neighbours(ui, coef, r)

    own_rows = range(HALO, HALO + ROWS)
    pending = []

    def send_block(src, above, below, ssem, rsem):
        copies = []
        for n, (dt, dst) in enumerate(((1, above), (-1, below))):
            c = pltpu.make_async_remote_copy(
                src_ref=src.at[own], dst_ref=dst, send_sem=ssem.at[n], recv_sem=rsem.at[n],
                device_id=at(0, dt), device_id_type=MESH,
            )
            c.start()
            copies.append(c)
        pending.extend(copies)
        return copies

    def send_g(ref, n):
        return send_block(
            ref, ref.at[pl.ds(0, HALO)], ref.at[pl.ds(HALO + ROWS, HALO)], mid_send.at[n], mid_recv.at[n]
        )

    def send_u(i):
        return send_block(
            u.at[i], uh.at[i, pl.ds(0, HALO)], uh.at[i, pl.ds(HALO, HALO)],
            ush_send.at[i], ush_recv.at[i],
        )

    def arrive(copies):
        for c in copies:
            c.wait_recv()

    def add_products(parts, i, gi, ui, gn):
        for r in own_rows:
            du = (diag[0, r] * ui[r])[:, :COLS]
            for k, ref in ((2 * i, gi), (2 * i + 1, gn)):
                term = du * ref[r][:, :COLS]
                parts[k] = term if parts[k] is None else parts[k] + term

    def moment_row(parts):
        lanes = lax.broadcasted_iota(jnp.int32, (1, 128), 1)
        row = jnp.zeros((1, 128), jnp.float32)
        for k, p in enumerate(parts):
            row = jnp.where(lanes == k, jnp.sum(p, axis=(0, 1), keepdims=True), row)
        return row

    def group_sum(buf, me, peers, n, ssem, rsem, beside=None):
        for d in peers:
            pltpu.make_async_remote_copy(
                src_ref=buf.at[me], dst_ref=buf.at[me], send_sem=ssem, recv_sem=rsem,
                device_id=d, device_id_type=MESH,
            ).start()
        most = buf.at[pl.ds(0, n - 1)]
        whole = pltpu.make_async_remote_copy(
            src_ref=most, dst_ref=most, send_sem=ssem, recv_sem=rsem,
            device_id=peers[0], device_id_type=MESH,
        )
        if beside is not None:
            beside()
        whole.wait_recv()
        pending.append(whole)
        total = buf[0]
        for i in range(1, n):
            total = total + buf[i]
        return total

    def all_sum(bufs, base, beside=(None, None, None)):
        c, p, w = bufs
        xy = y * 4 + x
        send, recv = sum_send.at, sum_recv.at
        p[xy] = group_sum(c, core, core_peer, 2, send[base], recv[base], beside[0])
        w[z] = group_sum(p, xy, plane_peers, 16, send[base + 1], recv[base + 1], beside[1])
        return group_sum(w, z, z_peers, 16, send[base + 2], recv[base + 2], beside[2])

    def coefficients(row):
        lanes = lax.broadcasted_iota(jnp.int32, (1, 128), 1)
        mu = [
            jnp.sum(jnp.where(lanes == k, row, 0.0), axis=(0, 1), keepdims=True) for k in range(6)
        ]
        return krylov_coefficients(mu)

    parts = [None] * 6
    iterate(g.at[0], u.at[0], g.at[1])
    moving = send_g(g.at[1], 0)
    shared = [send_u(0)]
    add_products(parts, 0, g.at[0], u.at[0], g.at[1])
    arrive(moving)
    iterate(g.at[1], u.at[1], g.at[2])
    moving = send_g(g.at[2], 1)
    shared.append(send_u(1))
    add_products(parts, 1, g.at[1], u.at[1], g.at[2])
    traded = {}

    def part_step(step, n):
        if step:
            arrive(traded[0, n])
        iterate(pg.at[step, n], pu.at[step, n], pg.at[step + 1, n])
        traded[step, n] = send_g(pg.at[step + 1, n], 2 + 4 * step + n)

    def source_part():
        arrive(halo[first:])
        for r in range(SPAN):
            ext[EARLY, r, :, COLS:] = jnp.where(slot < 64, early_r[r], early_l[r])
            pg[0, 0, r] = ext[EARLY, r] * diag[1, r]
        part_step(0, 0)

    def field_part(i):
        arrive(shared[i])
        for r in range(SPAN):
            if r in own_rows:
                v = u[i, r]
            else:
                v = uh[i, r if r < HALO else r - ROWS]
            pg[0, 1 + i, r] = ext[CAP, r] * diag[1, r] * v
        part_step(0, 1 + i)

    source_part()
    field_part(0)
    arrive(moving)
    iterate(g.at[2], u.at[2], z1)
    shared.append(send_u(2))
    add_products(parts, 2, g.at[2], u.at[2], z1)
    a0[core] = moment_row(parts).reshape(1, 1, 128)
    for c in loads[8:10]:
        c.wait()
    pl.semaphore_wait(reach.at[1], 2)

    def beside_plane():
        field_part(1)
        field_part(2)

    def beside_z():
        for n in (0, 1, 2, 3):
            part_step(1, n)

    row = all_sum((a0, a1, a2), 0, (None, beside_plane, beside_z))
    c1 = coefficients(row.reshape(1, 128))

    def added(ref, r):
        return ref[0, r] + c1[0] * ref[1, r] + c1[1] * ref[2, r] + c1[2] * ref[3, r]

    for n in range(4):
        arrive(traded[1, n])
    for r in range(SPAN):
        g[5, r] = added(pg.at[2], r)
    iterate(g.at[5], u.at[5], z1)
    held = jnp.zeros((LAYERS, COLS), jnp.float32)
    for r in own_rows:
        g[3, r] = added(pg.at[0], r)
        g[4, r] = added(pg.at[1], r)
        u[3, r] = added(pu.at[0], r)
        u[4, r] = added(pu.at[1], r)
        v = c1[0] * u[0, r] + c1[1] * u[1, r] + c1[2] * u[2, r]
        out_late[:, r - HALO, :] = v[:, :COLS]
        held = held + v[:, :COLS] * rate_late[:, r - HALO, :]
    stores = [
        pltpu.make_async_copy(src, dst, store_sem.at[n])
        for n, (src, dst) in enumerate(
            ((out_late, late_out), (out_early, early_out), (out_bank, bank_out))
        )
    ]
    stores[0].start()

    parts = [None] * 6
    add_products(parts, 0, g.at[3], u.at[3], g.at[4])
    add_products(parts, 1, g.at[4], u.at[4], g.at[5])
    add_products(parts, 2, g.at[5], u.at[5], z1)
    for c in loads[10:]:
        c.wait()
    moments = moment_row(parts)
    terms = [held]
    for i in (3, 4, 5):
        t = None
        for r in own_rows:
            w = u[i, r][:, :COLS] * rate_early[:, r - HALO, :]
            t = w if t is None else t + w
        terms.append(t)

    hi = lax.Precision.HIGHEST
    f32 = jnp.float32

    def iota(shape, dim):
        return lax.broadcasted_iota(jnp.int32, shape, dim)

    spread = (iota((16, 128), 0) == iota((16, 128), 1) % 16).astype(f32)
    bank_of = jnp.dot(bank[...].astype(f32), spread, precision=hi, preferred_element_type=f32)
    mine = iota((LAYERS, 128), 0) == iota((LAYERS, 128), 1) // 16
    bank_row = jnp.sum(jnp.where(mine, bank_of, 0.0), axis=0, keepdims=True)
    chosen = (iota((BANKS, 128), 0) == (bank_row + 0.5).astype(jnp.int32)).astype(f32)
    tile_of = (iota((COLS, 128), 0) // DCOLS == iota((COLS, 128), 1) % 16).astype(f32)
    tiles = jnp.dot(jnp.concatenate(terms, axis=0), tile_of, precision=hi, preferred_element_type=f32)
    tiles = jnp.where(iota((4 * LAYERS, 128), 0) % LAYERS == iota((4 * LAYERS, 128), 1) // 16, tiles, 0.0)
    sums = lax.dot_general(
        tiles, chosen, (((1,), (1,)), ((), ())), precision=hi, preferred_element_type=f32
    )
    for i in range(4):
        s = jnp.sum(sums[i * LAYERS : (i + 1) * LAYERS], axis=0, keepdims=True)
        b0[core, 2 * i] = s[:, :128]
        b0[core, 2 * i + 1] = s[:, 128:]
    b0[core, 8] = moments

    def settle():
        for c in halo + pending:
            c.wait_send()
        pending.clear()

    total = all_sum((b0, b1, b2), 3, (None, None, settle))
    c2 = coefficients(total[8])
    for h in range(2):
        out_bank[:, h * 128 : (h + 1) * 128] = (
            total[h] + c2[0] * total[2 + h] + c2[1] * total[4 + h] + c2[2] * total[6 + h]
        )
    for r in range(ROWS):
        e = HALO + r
        v = c2[0] * u[3, e] + c2[1] * u[4, e] + c2[2] * u[5, e]
        out_early[:, r, :] = v[:, :COLS]
    stores[1].start()
    stores[2].start()
    for c in pending:
        c.wait_send()
    for c in stores:
        c.wait()


def finish(late, early, bank, out_late, out_early, out_bank, late_v, early_v, bank_v, sem):
    ins = [
        pltpu.make_async_copy(src, dst, sem.at[n])
        for n, (src, dst) in enumerate(((late, late_v), (early, early_v), (bank, bank_v)))
    ]
    outs = [
        pltpu.make_async_copy(src, dst, sem.at[3 + n])
        for n, (src, dst) in enumerate(((late_v, out_late), (early_v, out_early), (bank_v, out_bank)))
    ]
    for c in ins:
        c.start()
    for c, d in zip(ins, outs):
        c.wait()
        d.start()
    for c in outs:
        c.wait()


def on_device(
    cond_x, cond_y, via_cond, capacity, class_map, via_mask, bank_map,
    source_late, source_early, rate_late, rate_early,
):
    f32, i32 = jnp.float32, jnp.int32
    hbm = pl.BlockSpec(memory_space=pltpu.HBM)
    dma = pltpu.SemaphoreType.DMA
    block = jax.ShapeDtypeStruct((LAYERS, ROWS, COLS), f32)
    shapes = (block, block, jax.ShapeDtypeStruct((1, BANKS), f32))
    wide = (SPAN, LAYERS, WIDE)
    field = pltpu.VMEM((LAYERS, ROWS, COLS), f32)
    results = pl.pallas_call(
        kernel,
        out_shape=shapes,
        in_specs=[hbm] * 11,
        out_specs=(hbm,) * 3,
        scratch_shapes=[
            field, field, pltpu.VMEM((1, BANKS), f32),
            field, field, field, field,
            pltpu.VMEM((ROWS, COLS), i32),
            pltpu.VMEM((LAYERS, NCLASS), i32),
            pltpu.VMEM((LAYERS, 16), i32),
            field, field, field, field,
            pltpu.VMEM((FIELDS,) + wide, f32),
            pltpu.VMEM((ROWS, LAYERS, 128), f32),
            pltpu.VMEM((ROWS, LAYERS, 128), f32),
            pltpu.VMEM((SPAN, LAYERS, 128), f32),
            pltpu.VMEM((SPAN, LAYERS, 128), f32),
            pltpu.VMEM((SPAN, LAYERS, 128), f32),
            pltpu.VMEM((SPAN, LAYERS, 128), f32),
            pltpu.VMEM((LAYERS, COLS), f32),
            pltpu.VMEM((LAYERS, 128), f32),
            pltpu.VMEM((LAYERS, 128), f32),
            pltpu.VMEM((6,) + wide, f32),
            pltpu.VMEM((2,) + wide, f32),
            pltpu.VMEM((6,) + wide, f32),
            pltpu.VMEM((6,) + wide, f32),
            pltpu.VMEM((3, 2 * HALO, LAYERS, WIDE), f32),
            pltpu.VMEM((3, 4) + wide, f32),
            pltpu.VMEM((2, 4) + wide, f32),
            pltpu.VMEM(wide, f32),
            pltpu.VMEM(wide, f32),
            pltpu.VMEM((2, 1, 1, 128), f32),
            pltpu.VMEM((16, 1, 1, 128), f32),
            pltpu.VMEM((16, 1, 1, 128), f32),
            pltpu.VMEM((2, 9, 1, 128), f32),
            pltpu.VMEM((16, 9, 1, 128), f32),
            pltpu.VMEM((16, 9, 1, 128), f32),
            dma((11,)),
            dma((3,)),
            dma((19,)),
            dma((19,)),
            dma((10, 2)),
            dma((10, 2)),
            dma((3, 2)),
            dma((3, 2)),
            dma((7,)),
            dma((7,)),
            pltpu.SemaphoreType.REGULAR((2,)),
        ],
        compiler_params=pltpu.CompilerParams(
            collective_id=0, has_side_effects=True, vmem_limit_bytes=60 << 20
        ),
        name="adjoint_steps",
    )(
        cond_x, cond_y, via_cond, capacity, class_map, via_mask, bank_map.reshape(LAYERS, 16),
        source_late, source_early, rate_late, rate_early,
    )
    late, early, bank = pl.pallas_call(
        finish,
        out_shape=shapes,
        in_specs=[hbm] * 3,
        out_specs=(hbm,) * 3,
        scratch_shapes=[field, field, pltpu.VMEM((1, BANKS), f32), dma((6,))],
        compiler_params=pltpu.CompilerParams(vmem_limit_bytes=60 << 20),
        name="write_results",
    )(*results)
    return late, early, bank.reshape(BANKS)


def solution(mesh):
    block = P(None, "tile", "layer")
    in_specs = (block,) * 4 + (P("tile", "layer"), P()) + (block,) * 5
    return jax.shard_map(
        on_device, mesh=mesh, in_specs=in_specs, out_specs=(block, block, P()), check_vma=False
    )
```
